256 devices in a mesh: dp: 32 (over x_lo, z, core), tm: 8 (over y, x_hi).
Axes of the slice: x: 4 (x_hi: 2, x_lo: 2; x = x_hi * 2 + x_lo), y: 4, z: 8, core: 2. Of those that a mesh axis runs over, the one named last changes fastest.
Arguments:
- clips: bfloat16 [32, 32, 16, 64, 128], P('dp', 'tm'), may hold values from -6 to 6
- cotangent: bfloat16 [32, 16, 8, 32, 256], P('dp', 'tm'), may hold values from -6 to 6
- clip_frames: int32 [32], P('dp'), may hold values from 1 to 32, 768 in all
- w_conv: bfloat16 [3, 3, 3, 128, 128], replicated, may hold values from -0.109375 to 0.109375
- w_down: bfloat16 [3, 3, 3, 128, 256], replicated, may hold values from -0.109375 to 0.109375
Outputs:
- encoded: bfloat16 [32, 16, 8, 32, 256], P('dp', 'tm')
- clip_grad: bfloat16 [32, 32, 16, 64, 128], P('dp', 'tm')
- conv_grad: float32 [3, 3, 3, 128, 128], replicated
- down_grad: float32 [3, 3, 3, 128, 256], replicated
The draws below stay inside these ranges and needn't reach their ends.
All inputs are finite; a program needn't handle non-finite values. No bound on the sum of `clip_frames` on one device may be relied on, other than what follows from the above.
Results may differ from the reference program's by a relative error of at most 0.013.
Values may be sent and summed in bfloat16 or wider, within the bound.
No kernel may reach another device: no remote copies, remote signals or barrier semaphores. Data moves between devices by JAX's collectives and lax.ppermute only.
A program may use at most 128 MiB of HBM per device.

```python
import math
import jax
import jax.numpy as jnp
import numpy as np
from jax import lax

C1 = 128
C2 = 256
H = 16
W = 64
CLIPS = 32
FRAMES = 32


def levels(stream_key, extent, shards, low, largest):
    loudness, own = 1.0, jax.random.fold_in(stream_key, 6)
    for axis_at, shards_of in shards:
        heights = jnp.exp(jax.random.uniform(jax.random.fold_in(own, axis_at), (shards_of,), jnp.float32, low / len(shards), largest / len(shards)))
        loudness = loudness * jnp.repeat(heights, extent[axis_at] // shards_of).reshape([-1 if axis == axis_at else 1 for axis in range(len(extent))])
    return loudness


def profile(number_of, total, bound, slope):
    portions = [(1 << 20) // math.isqrt(rank ** slope) + 1 for rank in range(2, number_of + 1)]
    rest, counts = total - bound - (number_of - 1), [1] * (number_of - 1)
    while rest > 0:
        candidates = [i for i in range(number_of - 1) if counts[i] < bound]
        whole, budget = sum([portions[i] for i in candidates]), rest
        for i in candidates:
            extra = min(bound - counts[i], max(1, budget * portions[i] // whole), rest)
            counts[i] = counts[i] + extra
            rest = rest - extra
    return np.array([bound] + counts)


def uneven_parts(key, amount, total, bound, skew):
    if amount == 2:
        one = jax.random.randint(key, (), max(1, total - bound), min(bound, total - 1) + 1)
        return jnp.stack([one, total - one])
    lengths = jnp.asarray(profile(amount, total, bound, skew), jnp.int32)
    twos = (amount - 1) // 2
    source_of, sink = lengths[1:1 + 2 * twos:2], lengths[2:2 + 2 * twos:2]
    room = jnp.minimum(source_of - 1, bound - sink)
    shifted = jax.random.randint(jax.random.fold_in(key, 1), (twos,), 0, 1 << 20) % (room + 1)
    lengths = lengths.at[1:1 + 2 * twos:2].set(source_of - shifted).at[2:2 + 2 * twos:2].set(sink + shifted)
    return lengths[jax.random.permutation(jax.random.fold_in(key, 2), amount)]


def gaussian(own_key, dims, spread, bound, split=(), held_as=jnp.bfloat16):
    drawn = spread * jax.random.normal(own_key, dims, jnp.float32)
    if split:
        drawn = drawn * levels(own_key, dims, split, -0.22, 0.18)
    return jnp.clip(drawn, -bound, bound).astype(held_as)


def setup_inputs(seed: int = 0) -> dict:
    seeds = jax.random.split(jax.random.key(seed), 6)
    return {
        "clips": gaussian(seeds[0], (CLIPS, FRAMES, H, W, C1), 1.0, 6.0, ((0, 32), (1, 8))),
        "cotangent": gaussian(seeds[1], (CLIPS, FRAMES // 2, H // 2, W // 2, C2), 1.0, 6.0, ((0, 32), (1, 8))),
        "clip_frames": uneven_parts(seeds[2], CLIPS, CLIPS * FRAMES * 3 // 4, FRAMES, 0).astype(jnp.int32),
        "w_conv": gaussian(seeds[3], (3, 3, 3, C1, C1), (27 * C1) ** -0.5, 0.109375),
        "w_down": gaussian(seeds[4], (3, 3, 3, C1, C2), (27 * C1) ** -0.5, 0.109375),
    }


LAYOUT = ('NDHWC', 'DHWIO', 'NDHWC')

def convolve(lhs, rhs, strides, padding, dilation):
    return lax.conv_general_dilated(lhs.astype(jnp.float32), rhs.astype(jnp.float32), strides, padding, lhs_dilation=dilation, dimension_numbers=LAYOUT, precision=lax.Precision.HIGHEST)

def flipped(weight):
    return jnp.swapaxes(weight[::-1, ::-1, ::-1], 3, 4)

def tap_sums(padded, grad, step):
    frames, rows, cols, chan_out = grad.shape
    chan_in = padded.shape[3]
    flat_grad = grad.reshape(-1, chan_out).astype(jnp.float32)
    terms = []
    for k in range(3):
        for a in range(3):
            for b in range(3):
                piece = lax.slice(padded, (k, a, b, 0), (k + step * (frames - 1) + 1, a + step * (rows - 1) + 1, b + step * (cols - 1) + 1, chan_in), (step, step, step, 1))
                terms.append(lax.dot_general(piece.reshape(-1, chan_in).astype(jnp.float32), flat_grad, (((0,), (0,)), ((), ())), precision=lax.Precision.HIGHEST))
    return jnp.stack(terms).reshape(3, 3, 3, chan_in, chan_out)

def reference(clips, cotangent, clip_frames, w_conv, w_down):

    def clip_pass(items):
        clip, cot, length = items
        x = clip[None]
        hidden = convolve(x, w_conv, (1, 1, 1), [(2, 0), (1, 1), (1, 1)], (1, 1, 1))
        act = jax.nn.silu(hidden).astype(jnp.bfloat16)
        encoded = convolve(act, w_down, (2, 2, 2), [(2, 0), (1, 1), (1, 1)], (1, 1, 1)).astype(jnp.bfloat16)
        times = jnp.arange(FRAMES // 2, dtype=jnp.int32)
        keep = (2 * times < length)[None, :, None, None, None]
        masked = jnp.where(keep, cot[None], jnp.zeros_like(cot[None]))
        act_grad = convolve(masked, flipped(w_down), (1, 1, 1), [(0, 3), (1, 2), (1, 2)], (2, 2, 2))
        sig = jax.nn.sigmoid(hidden)
        hidden_grad = (act_grad * sig * (1.0 + hidden * (1.0 - sig))).astype(jnp.bfloat16)
        clip_grad = convolve(hidden_grad, flipped(w_conv), (1, 1, 1), [(0, 2), (1, 1), (1, 1)], (1, 1, 1)).astype(jnp.bfloat16)
        xpad = jnp.pad(clip, ((2, 0), (1, 1), (1, 1), (0, 0)))
        apad = jnp.pad(act[0], ((2, 0), (1, 1), (1, 1), (0, 0)))
        down_part = tap_sums(apad, masked[0], 2)
        conv_part = tap_sums(xpad, hidden_grad[0], 1)
        return (encoded[0], clip_grad[0], conv_part, down_part)
    encoded, clip_grad, conv_parts, down_parts = lax.map(clip_pass, (clips, cotangent, clip_frames))
    scale = 1.0 / math.sqrt(CLIPS * FRAMES * H * W)
    conv_grad = lax.optimization_barrier(jnp.sum(conv_parts, axis=0)) * scale
    down_grad = lax.optimization_barrier(jnp.sum(down_parts, axis=0)) * scale
    return (encoded, clip_grad, conv_grad, down_grad)
```

```python
import math

import jax
import jax.numpy as jnp
from jax import lax
from jax.sharding import Mesh
from jax.sharding import PartitionSpec as P

LAYOUT = ("NDHWC", "DHWIO", "NDHWC")
TM = ("y", "xh")
DP = ("xl", "z", "c")
XY = ("xl", "xh", "y")


def shifted(block, distance):
    devices = range(8)
    route = [(i - distance, i) for i in devices if i - distance in devices]
    return lax.ppermute(block, TM, route)


def convolve(lhs, rhs, strides, padding, dilation):
    return lax.conv_general_dilated(
        lhs,
        rhs,
        strides,
        padding,
        lhs_dilation=dilation,
        dimension_numbers=LAYOUT,
        preferred_element_type=jnp.float32,
    )


def flipped(weight):
    return jnp.swapaxes(weight[::-1, ::-1, ::-1], 3, 4)


def kernel_sums(padded, grad, step):
    extent = [step * (grad.shape[d] - 1) + 3 for d in range(3)]
    trimmed = padded[: extent[0], : extent[1], : extent[2]]
    result = lax.conv_general_dilated(
        trimmed[None],
        grad[None],
        (1, 1, 1),
        "VALID",
        rhs_dilation=(step, step, step),
        dimension_numbers=("CDHWN", "IDHWO", "NDHWC"),
        preferred_element_type=jnp.float32,
    )
    return jnp.transpose(result, (1, 2, 3, 0, 4))


def exchange(value, axes):
    return lax.all_to_all(value, axes, 0, 0, tiled=True)


def add_up(value, parts):
    split = value.reshape((parts, value.shape[0] // parts, 128))
    return jnp.sum(split.astype(jnp.float32), axis=0).astype(jnp.bfloat16)


def gather(value, axes, parts):
    return exchange(jnp.tile(value, (parts, 1)), axes)


def total(rows):
    part = add_up(exchange(rows.astype(jnp.bfloat16), "c"), 2)
    part = add_up(exchange(part, XY), 16)
    part = add_up(gather(part, "z", 8), 8)
    return gather(gather(part, XY, 16), "c", 2)


def shards(clips, cotangent, clip_frames, w_conv, w_down):
    frames = clips.shape[1]
    rows = clips.shape[2]
    cols = clips.shape[3]
    spatial = [(1, 1), (1, 1)]
    before = shifted(clips[:, frames - 2 :], 1)
    x_ext = jnp.concatenate([before, clips], axis=1)
    hidden = convolve(x_ext, w_conv, (1, 1, 1), [(0, 0)] + spatial, (1, 1, 1))
    act = jax.nn.silu(hidden).astype(jnp.bfloat16)
    act_before = shifted(act[:, frames - 2 :], 1)
    act_ext = jnp.concatenate([act_before, act], axis=1)
    encoded = convolve(act_ext, w_down, (2, 2, 2), [(0, 0)] + spatial, (1, 1, 1)).astype(
        jnp.bfloat16
    )
    times = lax.axis_index(TM) * (frames // 2) + jnp.arange(frames // 2, dtype=jnp.int32)
    keep = (2 * times < clip_frames[0])[None, :, None, None, None]
    masked = jnp.where(keep, cotangent, jnp.zeros_like(cotangent))
    scale = 1.0 / math.sqrt(lax.axis_size(DP) * frames * lax.axis_size(TM) * rows * cols)
    act_grad_ext = convolve(masked, flipped(w_down), (1, 1, 1), [(2, 3), (1, 2), (1, 2)], (2, 2, 2))
    returned = shifted(act_grad_ext[:, :2], -1)
    act_grad = act_grad_ext[:, 2:] + jnp.pad(
        returned, ((0, 0), (frames - 2, 0), (0, 0), (0, 0), (0, 0))
    )
    sig = jax.nn.sigmoid(hidden)
    hidden_grad = (act_grad * sig * (1.0 + hidden * (1.0 - sig))).astype(jnp.bfloat16)
    apad = jnp.pad(act_ext[0], ((0, 0), (1, 1), (1, 1), (0, 0)))
    down_local = kernel_sums(apad, masked[0], 2)
    clip_grad_ext = convolve(hidden_grad, flipped(w_conv), (1, 1, 1), [(2, 2)] + spatial, (1, 1, 1))
    back = shifted(clip_grad_ext[:, :2].astype(jnp.bfloat16), -1).astype(jnp.float32)
    clip_grad = (
        clip_grad_ext[:, 2:] + jnp.pad(back, ((0, 0), (frames - 2, 0), (0, 0), (0, 0), (0, 0)))
    ).astype(jnp.bfloat16)
    xpad = jnp.pad(x_ext[0], ((0, 0), (1, 1), (1, 1), (0, 0)))
    conv_local = kernel_sums(xpad, hidden_grad[0], 1)
    down_rows = jnp.concatenate(
        [down_local[..., :128].reshape(-1, 128), down_local[..., 128:].reshape(-1, 128)]
    )
    down_sum = total(jnp.pad(down_rows, ((0, 256), (0, 0))))
    conv_sum = total(jnp.pad(conv_local.reshape(-1, 128), ((0, 128), (0, 0))))
    conv_sum = conv_sum[:3456].reshape(3, 3, 3, 128, 128).astype(jnp.float32)
    down_sum = jnp.concatenate(
        [
            down_sum[:3456].reshape(3, 3, 3, 128, 128),
            down_sum[3456:6912].reshape(3, 3, 3, 128, 128),
        ],
        axis=-1,
    ).astype(jnp.float32)
    return (encoded, clip_grad, conv_sum * scale, down_sum * scale)


def solution(mesh):
    fine = Mesh(mesh.devices.reshape(2, 8, 2, 4, 2), DP + TM)
    spread = P(DP, TM, None, None, None)
    in_specs = (spread, spread, P(DP), P(), P())
    out_specs = (spread, spread, P(), P())
    return jax.shard_map(shards, mesh=fine, in_specs=in_specs, out_specs=out_specs, check_vma=False)
```

```python
import functools
import math

import jax
import jax.numpy as jnp
from jax import lax
from jax.experimental import pallas as pl
from jax.experimental.pallas import tpu as pltpu
from jax.sharding import Mesh
from jax.sharding import PartitionSpec as P

TM = ("y", "xh")
DP = ("xl", "z", "c")
XY = ("xl", "xh", "y")

BF = jnp.bfloat16
F32 = jnp.float32
VMEM = pl.BlockSpec(memory_space=pltpu.VMEM)
SMEM = pl.BlockSpec(memory_space=pltpu.SMEM)
ANY = pl.BlockSpec(memory_space=pl.ANY)
HALF = 42 * 128


def params(mib):
    return pltpu.CompilerParams(vmem_limit_bytes=mib * 1024 * 1024)


def cost(flops, moved):
    return pl.CostEstimate(flops=flops, bytes_accessed=moved, transcendentals=0)


def dot(a, b):
    return jnp.dot(a, b, preferred_element_type=F32)


def turned(v):
    return v.astype(F32).T.astype(BF)


def column(shape):
    return lax.broadcasted_iota(jnp.int32, shape, 1)


def from_left(v):
    return jnp.where(column(v.shape) == 0, 0.0, pltpu.roll(v, 1, 1))


def from_right(v):
    last = v.shape[1] - 1
    return jnp.where(column(v.shape) == last, 0.0, pltpu.roll(v, last, 1))


def spread(dst, frame, even, odd):
    dst[frame, 1:17, :, 0:128] = even.astype(BF)
    dst[frame, 1:17, :, 128:256] = odd.astype(BF)
    dst[frame, 1:17, :, 256:384] = from_left(odd).astype(BF)
    dst[frame, 1:17, :, 384:512] = from_right(even).astype(BF)


def split_columns(wide, v):
    wide[...] = v.astype(F32)
    return wide[:, pl.ds(0, 32, stride=2), :], wide[:, pl.ds(1, 32, stride=2), :]


def clear_edges(dst, frames):
    z = jnp.zeros((frames, 1, 32, 512), BF)
    dst[:, 0:1] = z
    dst[:, 17:18] = z


def conv_frame(src, f, w_ref):
    acc = None
    for k in range(3):
        for a in range(3):
            lhs = src[f + k, a : a + 16].reshape(512, 512)
            term = dot(lhs, w_ref[3 * k + a])
            acc = term if acc is None else acc + term
    return acc


def pair_weights(dst, tap, w):
    z = jnp.zeros((128, 128), BF)
    rows = ((w[1], w[0]), (w[2], w[1]), (w[0], z), (z, w[2]))
    for r, (even, odd) in enumerate(rows):
        dst[tap, 128 * r : 128 * r + 128, 0:128] = even
        dst[tap, 128 * r : 128 * r + 128, 128:256] = odd


def kernel_weights(wconv_ref, wdown_ref, wc_ref, wa_ref):
    z = jnp.zeros((256, 128), BF)
    for tap in range(9):
        pair_weights(wc_ref, tap, [wconv_ref[3 * tap + b] for b in range(3)])
        w = [turned(wdown_ref[tap, 128 * b : 128 * b + 128]) for b in range(3)]
        wa_ref[tap, 0:256, 0:128] = w[1]
        wa_ref[tap, 0:256, 128:256] = w[2]
        wa_ref[tap, 256:512, 0:128] = z
        wa_ref[tap, 256:512, 128:256] = w[0]


def call_weights(w_conv, w_down):
    return pl.pallas_call(
        kernel_weights,
        out_shape=(jax.ShapeDtypeStruct((9, 512, 256), BF),) * 2,
        in_specs=[VMEM, VMEM],
        out_specs=(VMEM, VMEM),
        compiler_params=params(16),
        cost_estimate=cost(10**6, 8 * 10**6),
    )(w_conv, w_down)


TERMS = {0: ((0, 2), (1, 0)), 1: ((1, 1),), 2: ((1, 2), (2, 0)), 3: ((2, 1),)}


def kernel_grads(core_ref, x_ref, before_ref, m_ref, next_ref, wc_ref, wa_ref, wd_ref,
                 hg_ref, own_ref, other_ref, enc_ref, part_ref,
                 wide, xs, ms, mt, acs, hgt, dact, sums, sems):
    core = core_ref[0]
    clear_edges(xs, 6)
    for f in range(6):
        frame = before_ref[f] if f < 2 else x_ref[f - 2]
        spread(xs, f, *split_columns(wide.at[f % 2], frame))
    ms[:, 8:9] = jnp.zeros((3, 1, 32, 512), BF)
    for t in range(3):
        m = next_ref[0] if t == 2 else m_ref[t]
        ms[t, 0:8, :, 0:256] = m
        ms[t, 0:8, :, 256:512] = from_right(m.astype(F32)).astype(BF)
        mt[:, 256 * t : 256 * t + 256] = turned(m.reshape(256, 256))
    acs[:, 0:1, 0:1] = jnp.zeros((4, 1, 1, 32, 384), BF)
    acs[:, 8:9, 1:2] = jnp.zeros((4, 1, 1, 32, 384), BF)
    sums[1, HALF - 384 :] = jnp.zeros((384, 128), BF)

    for f in range(4):
        even = odd = None
        for t, k in TERMS[f]:
            here = ms[t, 0:8].reshape(256, 512)
            below = ms[t, 1:9].reshape(256, 512)
            e = dot(here, wa_ref[3 * k + 1])
            o = dot(here, wa_ref[3 * k + 2]) + dot(below, wa_ref[3 * k])
            even = e if even is None else even + e
            odd = o if odd is None else odd + o
        dact[f, :, 0] = even.reshape(8, 32, 256)
        dact[f, :, 1] = odd.reshape(8, 32, 256)

    for f in range(4):
        hidden = conv_frame(xs, f, wc_ref)
        sig = 1.0 / (1.0 + jnp.exp(-hidden))
        act = (hidden * sig).reshape(8, 2, 32, 256)
        left = from_left(act[..., 128:256].reshape(16, 32, 128)).reshape(8, 2, 32, 128)
        actb = act.astype(BF)
        leftb = left.astype(BF)
        acs[f, 0:8, 1, :, 128:384] = actb[:, 0]
        acs[f, 1:9, 0, :, 128:384] = actb[:, 1]
        acs[f, 0:8, 1, :, 0:128] = leftb[:, 0]
        acs[f, 1:9, 0, :, 0:128] = leftb[:, 1]
        grad = dact[f].reshape(512, 256) * sig * (1.0 + hidden * (1.0 - sig))
        hg_ref[f] = grad.astype(BF).reshape(16, 32, 256)
        hgt[:, 512 * f : 512 * f + 512] = grad.T.astype(BF)

    def put(block, v):
        half, at = divmod(128 * block, HALF)
        sums[half, at : at + 128] = v

    def tap(f, a):
        rows = (acs[f, 0:8, 0], acs[f, 0:8, 1], acs[f, 1:9, 0])[a]
        return rows.reshape(256, 384)

    for k in range(3):
        m_t = mt[:, 0:512] if k == 2 else mt[:, 256:768]
        parity = 1 if k == 1 else 0
        for a in range(3):
            right = jnp.concatenate([tap(parity, a), tap(parity + 2, a)], axis=0)
            g = dot(m_t, right)
            for b in range(3):
                block = g[:, 128 * b : 128 * b + 128].T.astype(BF)
                put(27 + 9 * k + 3 * a + b, block[:, 0:128])
                put(54 + 9 * k + 3 * a + b, block[:, 128:256])

    for k in range(3):
        for a in range(3):
            right = xs[k : k + 4, a : a + 16].reshape(2048, 512)
            g = dot(hgt[...], right)
            for b in range(3):
                u, v = (2, 0, 1)[b], (0, 1, 3)[b]
                both = g[0:128, 128 * u : 128 * u + 128] + g[128:256, 128 * v : 128 * v + 128]
                put(9 * k + 3 * a + b, both.T.astype(BF))

    send = pltpu.make_async_copy(sums.at[1 - core], other_ref, sems.at[0])
    keep = pltpu.make_async_copy(sums.at[core], own_ref, sems.at[1])
    send.start()
    keep.start()
    for t in range(3):
        acc = None
        for k in range(3):
            f = 2 * t + k - 2
            if 0 <= f < 4:
                for a in range(3):
                    term = dot(tap(f, a), wd_ref[3 * k + a])
                    acc = term if acc is None else acc + term
        if t == 2:
            part_ref[0] = acc.reshape(8, 32, 256)
        else:
            enc_ref[t] = acc.reshape(8, 32, 256)
    send.wait()
    keep.wait()


def call_grads(core, x, before, m, after, wc, wa, wd):
    return pl.pallas_call(
        kernel_grads,
        out_shape=(
            jax.ShapeDtypeStruct((4, 16, 32, 256), BF),
            jax.ShapeDtypeStruct((HALF, 128), BF),
            jax.ShapeDtypeStruct((HALF, 128), BF),
            jax.ShapeDtypeStruct((2, 8, 32, 256), F32),
            jax.ShapeDtypeStruct((1, 8, 32, 256), F32),
        ),
        in_specs=[SMEM] + [VMEM] * 7,
        out_specs=(VMEM, ANY, ANY, VMEM, VMEM),
        scratch_shapes=[
            pltpu.VMEM((2, 16, 64, 128), F32),
            pltpu.VMEM((6, 18, 32, 512), BF),
            pltpu.VMEM((3, 9, 32, 512), BF),
            pltpu.VMEM((256, 768), BF),
            pltpu.VMEM((4, 9, 2, 32, 384), BF),
            pltpu.VMEM((256, 2048), BF),
            pltpu.VMEM((4, 8, 2, 32, 256), F32),
            pltpu.VMEM((2, HALF, 128), BF),
            pltpu.SemaphoreType.DMA((2,)),
        ],
        compiler_params=params(40),
        cost_estimate=cost(12 * 10**9, 10**7),
    )(core, x, before, m, after, wc, wa, wd)


def kernel_clip(h_ref, after_ref, w_ref, out_ref, hs, wt, wide):
    clear_edges(hs, 6)
    for tap in range(9):
        pair_weights(wt, tap, [turned(w_ref[3 * (8 - tap) + 2 - b]) for b in range(3)])
    for f in range(6):
        v = (h_ref[f] if f < 4 else after_ref[f - 4]).astype(F32)
        spread(hs, f, v[:, :, 0:128], v[:, :, 128:256])
    for f in range(4):
        v = conv_frame(hs, f, wt).reshape(16, 32, 256)
        wide[f % 2, :, pl.ds(0, 32, stride=2), :] = v[:, :, 0:128]
        wide[f % 2, :, pl.ds(1, 32, stride=2), :] = v[:, :, 128:256]
        out_ref[f] = wide[f % 2].astype(BF)


def call_clip(h, after, w):
    return pl.pallas_call(
        kernel_clip,
        out_shape=jax.ShapeDtypeStruct((4, 16, 64, 128), BF),
        in_specs=[VMEM] * 3,
        out_specs=VMEM,
        scratch_shapes=[
            pltpu.VMEM((6, 18, 32, 512), BF),
            pltpu.VMEM((9, 512, 256), BF),
            pltpu.VMEM((2, 16, 64, 128), F32),
        ],
        compiler_params=params(32),
        cost_estimate=cost(5 * 10**9, 5 * 10**6),
    )(h, after, w)


def kernel_out(scale, core_ref, own_ref, other_ref, conv_ref, down_ref):
    def write(halves):
        for block in range(81):
            half, at = divmod(128 * block, HALF)
            v = halves[half][at : at + 128].astype(F32) * scale
            which, tap = divmod(block, 27)
            if which == 0:
                conv_ref[tap] = v
            else:
                down_ref[tap, :, 128 * (which - 1) : 128 * which] = v

    @pl.when(core_ref[0] == 0)
    def _():
        write((own_ref, other_ref))

    @pl.when(core_ref[0] == 1)
    def _():
        write((other_ref, own_ref))


def call_out(core, own, other, scale):
    return pl.pallas_call(
        functools.partial(kernel_out, scale),
        out_shape=(
            jax.ShapeDtypeStruct((27, 128, 128), F32),
            jax.ShapeDtypeStruct((27, 128, 256), F32),
        ),
        in_specs=[SMEM, VMEM, VMEM],
        out_specs=(VMEM, VMEM),
        compiler_params=params(32),
        cost_estimate=cost(10**6, 8 * 10**6),
    )(core, own, other)


def shifted(block, distance):
    devices = range(8)
    route = [(i - distance, i) for i in devices if i - distance in devices]
    return lax.ppermute(block, TM, route)


def swapped(block):
    return lax.ppermute(block, "c", [(0, 1), (1, 0)])


def exchange(value, axes):
    return lax.all_to_all(value, axes, 0, 0, tiled=True)


def add_up(value, parts):
    split = value.reshape((parts, value.shape[0] // parts, 128))
    return jnp.sum(split.astype(F32), axis=0).astype(BF)


def gather(value, axes, parts):
    return exchange(jnp.tile(value, (parts, 1)), axes)


def shards(clips, cotangent, clip_frames, w_conv, w_down):
    frames, rows, cols = clips.shape[1:4]
    core = lax.axis_index("c").astype(jnp.int32).reshape(1)
    last = clips[0, 2:]
    before = shifted(last, 1)
    cotangent, _ = lax.optimization_barrier((cotangent, last))
    times = lax.axis_index(TM) * 2 + jnp.arange(2, dtype=jnp.int32)
    keep = (2 * times < clip_frames[0])[:, None, None, None]
    masked = jnp.where(keep, cotangent[0], jnp.zeros_like(cotangent[0]))
    masked_after = shifted(masked[:1], -1)
    taps_conv = w_conv.reshape(27, 128, 128)
    taps_down = w_down.reshape(9, 384, 256)
    wc, wa = call_weights(taps_conv, taps_down)
    hg, own, other, enc, part = call_grads(
        core, clips[0], before, masked, masked_after, wc, wa, taps_down
    )
    own = (own.astype(F32) + swapped(other).astype(F32)).astype(BF)
    own = add_up(exchange(own, XY), 16)
    own, ends, part = lax.optimization_barrier((own, hg[:2], part))
    after = shifted(ends, -1)
    part = shifted(part, 1)
    own = add_up(gather(own, "z", 8), 8)
    own, after, part = lax.optimization_barrier((own, after, part))
    own = gather(own, XY, 16)
    clip_grad = call_clip(hg, after, taps_conv)[None]
    own, clip_grad = lax.optimization_barrier((own, clip_grad))
    encoded = jnp.concatenate([enc[:1] + part, enc[1:]]).astype(BF)[None]
    scale = 1.0 / math.sqrt(lax.axis_size(DP) * frames * lax.axis_size(TM) * rows * cols)
    conv_grad, down_grad = call_out(core, own, swapped(own), scale)
    return (encoded, clip_grad, conv_grad.reshape(w_conv.shape), down_grad.reshape(w_down.shape))


def solution(mesh):
    fine = Mesh(mesh.devices.reshape(2, 8, 2, 4, 2), DP + TM)
    spread_out = P(DP, TM, None, None, None)
    in_specs = (spread_out, spread_out, P(DP), P(), P())
    out_specs = (spread_out, spread_out, P(), P())
    return jax.shard_map(shards, mesh=fine, in_specs=in_specs, out_specs=out_specs, check_vma=False)
```

```python
import functools
import math

import jax
import jax.numpy as jnp
from jax import lax
from jax.experimental import pallas as pl
from jax.experimental.pallas import tpu as pltpu
from jax.sharding import Mesh
from jax.sharding import PartitionSpec as P

TM = ("y", "xh")
DP = ("xl", "zh", "zl", "c")
NEAR = ("xl", "xh", "y", "zl")

BF = jnp.bfloat16
F32 = jnp.float32
VMEM = pl.BlockSpec(memory_space=pltpu.VMEM)
SMEM = pl.BlockSpec(memory_space=pltpu.SMEM)
ANY = pl.BlockSpec(memory_space=pl.ANY)
HBM = pl.BlockSpec(memory_space=pltpu.HBM)
HALF = 42 * 128
EARLY = 7


def params(mib):
    return pltpu.CompilerParams(vmem_limit_bytes=mib * 1024 * 1024)


def cost(flops, moved):
    return pl.CostEstimate(flops=flops, bytes_accessed=moved, transcendentals=0)


def dot(a, b):
    return jnp.dot(a, b, preferred_element_type=F32)


def turned(v):
    return v.astype(F32).T.astype(BF)


def column(shape):
    return lax.broadcasted_iota(jnp.int32, shape, 1)


def from_left(v):
    return jnp.where(column(v.shape) == 0, 0.0, pltpu.roll(v, 1, 1))


def from_right(v):
    last = v.shape[1] - 1
    return jnp.where(column(v.shape) == last, 0.0, pltpu.roll(v, last, 1))


def spread(dst, frame, even, odd):
    dst[frame, 1:17, :, 0:128] = even.astype(BF)
    dst[frame, 1:17, :, 128:256] = odd.astype(BF)
    dst[frame, 1:17, :, 256:384] = from_left(odd).astype(BF)
    dst[frame, 1:17, :, 384:512] = from_right(even).astype(BF)


def split_columns(wide, v):
    wide[...] = v.astype(F32)
    return wide[:, pl.ds(0, 32, stride=2), :], wide[:, pl.ds(1, 32, stride=2), :]


def clear_edges(dst, frames):
    z = jnp.zeros((frames, 1, 32, 512), BF)
    dst[:, 0:1] = z
    dst[:, 17:18] = z


def conv_frame(src, f, w_ref):
    acc = None
    for k in range(3):
        for a in range(3):
            lhs = src[f + k, a : a + 16].reshape(512, 512)
            term = dot(lhs, w_ref[3 * k + a])
            acc = term if acc is None else acc + term
    return acc


def pair_weights(dst, tap, w):
    z = jnp.zeros((128, 128), BF)
    rows = ((w[1], w[0]), (w[2], w[1]), (w[0], z), (z, w[2]))
    for r, (even, odd) in enumerate(rows):
        dst[tap, 128 * r : 128 * r + 128, 0:128] = even
        dst[tap, 128 * r : 128 * r + 128, 128:256] = odd


def kernel_weights(x_ref, wconv_ref, wdown_ref, wc_ref, wa_ref, late_ref, wide, xs):
    z = jnp.zeros((256, 128), BF)
    for tap in range(9):
        pair_weights(wc_ref, tap, [wconv_ref[3 * tap + b] for b in range(3)])
        w = [turned(wdown_ref[tap, 128 * b : 128 * b + 128]) for b in range(3)]
        wa_ref[tap, 0:256, 0:128] = w[1]
        wa_ref[tap, 0:256, 128:256] = w[2]
        wa_ref[tap, 256:512, 0:128] = z
        wa_ref[tap, 256:512, 128:256] = w[0]
    clear_edges(xs, 4)
    for f in range(4):
        spread(xs, f, *split_columns(wide.at[f % 2], x_ref[f]))
    for f in range(2):
        late_ref[f] = conv_frame(xs, f, wc_ref)


def call_weights(x, w_conv, w_down):
    return pl.pallas_call(
        kernel_weights,
        out_shape=(jax.ShapeDtypeStruct((9, 512, 256), BF),) * 2
        + (jax.ShapeDtypeStruct((2, 512, 256), F32),),
        in_specs=[VMEM] * 3,
        out_specs=(VMEM,) * 3,
        scratch_shapes=[
            pltpu.VMEM((2, 16, 64, 128), F32),
            pltpu.VMEM((4, 18, 32, 512), BF),
        ],
        compiler_params=params(16),
        cost_estimate=cost(10**6, 8 * 10**6),
    )(x, w_conv, w_down)


TERMS = {0: ((0, 2), (1, 0)), 1: ((1, 1),), 2: ((1, 2), (2, 0)), 3: ((2, 1),)}


def kernel_grads(core_ref, x_ref, before_ref, m_ref, next_ref, wc_ref, wa_ref, late_ref, wd_ref,
                 hg_ref, own_ref, other_ref, enc_ref, part_ref,
                 wide, xs, ms, mt, acs, hgt, dact, sums, sems):
    core = core_ref[0]
    clear_edges(xs, 6)
    for f in range(6):
        frame = before_ref[f] if f < 2 else x_ref[f - 2]
        spread(xs, f, *split_columns(wide.at[f % 2], frame))
    ms[:, 8:9] = jnp.zeros((3, 1, 32, 512), BF)
    for t in range(3):
        m = next_ref[0] if t == 2 else m_ref[t]
        ms[t, 0:8, :, 0:256] = m
        ms[t, 0:8, :, 256:512] = from_right(m.astype(F32)).astype(BF)
        mt[:, 256 * t : 256 * t + 256] = turned(m.reshape(256, 256))
    acs[:, 0:1, 0:1] = jnp.zeros((4, 1, 1, 32, 384), BF)
    acs[:, 8:9, 1:2] = jnp.zeros((4, 1, 1, 32, 384), BF)
    sums[0, HALF - 128 :] = jnp.zeros((128, 128), BF)
    sums[1, HALF - 256 :] = jnp.zeros((256, 128), BF)

    for f in range(4):
        even = odd = None
        for t, k in TERMS[f]:
            here = ms[t, 0:8].reshape(256, 512)
            below = ms[t, 1:9].reshape(256, 512)
            e = dot(here, wa_ref[3 * k + 1])
            o = dot(here, wa_ref[3 * k + 2]) + dot(below, wa_ref[3 * k])
            even = e if even is None else even + e
            odd = o if odd is None else odd + o
        dact[f, :, 0] = even.reshape(8, 32, 256)
        dact[f, :, 1] = odd.reshape(8, 32, 256)

    for f in range(4):
        hidden = conv_frame(xs, f, wc_ref) if f < 2 else late_ref[f - 2]
        sig = 1.0 / (1.0 + jnp.exp(-hidden))
        act = (hidden * sig).reshape(8, 2, 32, 256)
        left = from_left(act[..., 128:256].reshape(16, 32, 128)).reshape(8, 2, 32, 128)
        actb = act.astype(BF)
        leftb = left.astype(BF)
        acs[f, 0:8, 1, :, 128:384] = actb[:, 0]
        acs[f, 1:9, 0, :, 128:384] = actb[:, 1]
        acs[f, 0:8, 1, :, 0:128] = leftb[:, 0]
        acs[f, 1:9, 0, :, 0:128] = leftb[:, 1]
        grad = dact[f].reshape(512, 256) * sig * (1.0 + hidden * (1.0 - sig))
        hg_ref[f] = grad.astype(BF).reshape(16, 32, 256)
        hgt[:, 512 * f : 512 * f + 512] = grad.T.astype(BF)

    def put(half, block, v):
        sums[half, 128 * block : 128 * block + 128] = v

    def tap(f, a):
        rows = (acs[f, 0:8, 0], acs[f, 0:8, 1], acs[f, 1:9, 0])[a]
        return rows.reshape(256, 384)

    for k in range(3):
        m_t = mt[:, 0:512] if k == 2 else mt[:, 256:768]
        parity = 1 if k == 1 else 0
        for a in range(3):
            right = jnp.concatenate([tap(parity, a), tap(parity + 2, a)], axis=0)
            g = dot(m_t, right)
            for b in range(3):
                block = g[:, 128 * b : 128 * b + 128].T.astype(BF)
                at = 9 * k + 3 * a + b
                half, first = (0, 27 + 2 * at) if at < EARLY else (1, 2 * (at - EARLY))
                put(half, first, block[:, 0:128])
                put(half, first + 1, block[:, 128:256])

    for k in range(3):
        for a in range(3):
            right = xs[k : k + 4, a : a + 16].reshape(2048, 512)
            g = dot(hgt[...], right)
            for b in range(3):
                u, v = (2, 0, 1)[b], (0, 1, 3)[b]
                both = g[0:128, 128 * u : 128 * u + 128] + g[128:256, 128 * v : 128 * v + 128]
                put(0, 9 * k + 3 * a + b, both.T.astype(BF))

    send = pltpu.make_async_copy(sums.at[1 - core], other_ref, sems.at[0])
    keep = pltpu.make_async_copy(sums.at[core], own_ref, sems.at[1])
    send.start()
    keep.start()
    for t in range(3):
        acc = None
        for k in range(3):
            f = 2 * t + k - 2
            if 0 <= f < 4:
                for a in range(3):
                    term = dot(tap(f, a), wd_ref[3 * k + a])
                    acc = term if acc is None else acc + term
        if t == 2:
            part_ref[0] = acc.astype(BF).reshape(8, 32, 256)
        else:
            enc_ref[t] = acc.reshape(8, 32, 256)
    send.wait()
    keep.wait()


def call_grads(core, x, before, m, after, wc, wa, late, wd):
    return pl.pallas_call(
        kernel_grads,
        out_shape=(
            jax.ShapeDtypeStruct((4, 16, 32, 256), BF),
            jax.ShapeDtypeStruct((HALF, 128), BF),
            jax.ShapeDtypeStruct((HALF, 128), BF),
            jax.ShapeDtypeStruct((2, 8, 32, 256), F32),
            jax.ShapeDtypeStruct((1, 8, 32, 256), BF),
        ),
        in_specs=[SMEM] + [VMEM] * 8,
        out_specs=(VMEM, ANY, ANY, VMEM, VMEM),
        scratch_shapes=[
            pltpu.VMEM((2, 16, 64, 128), F32),
            pltpu.VMEM((6, 18, 32, 512), BF),
            pltpu.VMEM((3, 9, 32, 512), BF),
            pltpu.VMEM((256, 768), BF),
            pltpu.VMEM((4, 9, 2, 32, 384), BF),
            pltpu.VMEM((256, 2048), BF),
            pltpu.VMEM((4, 8, 2, 32, 256), F32),
            pltpu.VMEM((2, HALF, 128), BF),
            pltpu.SemaphoreType.DMA((2,)),
        ],
        compiler_params=params(40),
        cost_estimate=cost(12 * 10**9, 10**7),
    )(core, x, before, m, after, wc, wa, late, wd)


def kernel_clip(h_ref, after_ref, w_ref, own_ref, part_ref, out_ref, enc_ref, hs, wt, wide):
    enc_ref[0] = (own_ref[0] + part_ref[0].astype(F32)).astype(BF)
    enc_ref[1] = own_ref[1].astype(BF)
    clear_edges(hs, 6)
    for tap in range(9):
        pair_weights(wt, tap, [turned(w_ref[3 * (8 - tap) + 2 - b]) for b in range(3)])
    for f in range(6):
        v = (h_ref[f] if f < 4 else after_ref[f - 4]).astype(F32)
        spread(hs, f, v[:, :, 0:128], v[:, :, 128:256])
    for f in range(4):
        v = conv_frame(hs, f, wt).reshape(16, 32, 256)
        wide[f % 2, :, pl.ds(0, 32, stride=2), :] = v[:, :, 0:128]
        wide[f % 2, :, pl.ds(1, 32, stride=2), :] = v[:, :, 128:256]
        out_ref[f] = wide[f % 2].astype(BF)


def call_clip(h, after, w, enc, part):
    return pl.pallas_call(
        kernel_clip,
        out_shape=(
            jax.ShapeDtypeStruct((4, 16, 64, 128), BF),
            jax.ShapeDtypeStruct((2, 8, 32, 256), BF),
        ),
        in_specs=[VMEM] * 5,
        out_specs=(VMEM, VMEM),
        scratch_shapes=[
            pltpu.VMEM((6, 18, 32, 512), BF),
            pltpu.VMEM((9, 512, 256), BF),
            pltpu.VMEM((2, 16, 64, 128), F32),
        ],
        compiler_params=params(32),
        cost_estimate=cost(5 * 10**9, 5 * 10**6),
    )(h, after, w, enc, part)


def write_half(half, scale, src, conv_ref, down_ref, conv, down, sems):
    def block(at):
        return src[128 * at : 128 * at + 128].astype(F32) * scale

    @pl.when(half == 0)
    def _():
        for at in range(27):
            conv[at] = block(at)
        to_conv = pltpu.make_async_copy(conv, conv_ref, sems.at[0])
        to_conv.start()
        for at in range(EARLY):
            down[at, :, 0:128] = block(27 + 2 * at)
            down[at, :, 128:256] = block(28 + 2 * at)
        to_down = pltpu.make_async_copy(down.at[0:EARLY], down_ref.at[0:EARLY], sems.at[1])
        to_down.start()
        to_conv.wait()
        to_down.wait()

    @pl.when(half == 1)
    def _():
        pieces = ((0, 7), (7, 14), (14, 27 - EARLY))
        copies = []
        for i, (first, last) in enumerate(pieces):
            for at in range(first, last):
                down[at, :, 0:128] = block(2 * at)
                down[at, :, 128:256] = block(2 * at + 1)
            target = down_ref.at[EARLY + first : EARLY + last]
            copies.append(pltpu.make_async_copy(down.at[first:last], target, sems.at[i]))
            copies[-1].start()
        for copy in copies:
            copy.wait()


def kernel_own(scale, core_ref, src, conv_ref, down_ref, conv, down, sems):
    write_half(core_ref[0], scale, src, conv_ref, down_ref, conv, down, sems)


def kernel_other(scale, core_ref, src, conv_in, down_in, conv_ref, down_ref, conv, down, sems):
    write_half(1 - core_ref[0], scale, src, conv_ref, down_ref, conv, down, sems)


def call_out(kernel, core, half, scale, begun=()):
    return pl.pallas_call(
        functools.partial(kernel, scale),
        out_shape=(pltpu.HBM((27, 128, 128), F32), pltpu.HBM((27, 128, 256), F32)),
        in_specs=[SMEM, VMEM] + [HBM] * len(begun),
        out_specs=(HBM, HBM),
        input_output_aliases={2: 0, 3: 1} if begun else {},
        scratch_shapes=[
            pltpu.VMEM((27, 128, 128), F32),
            pltpu.VMEM((27 - EARLY, 128, 256), F32),
            pltpu.SemaphoreType.DMA((3,)),
        ],
        compiler_params=params(16),
        cost_estimate=cost(10**6, 4 * 10**6),
    )(core, half, *begun)


CHUNK = HALF // 32


def kernel_fold(in_ref, out_ref):
    total = in_ref[0].astype(F32)
    for i in range(1, in_ref.shape[0]):
        total += in_ref[i].astype(F32)
    total = total.astype(BF)
    for i in range(out_ref.shape[0]):
        out_ref[i] = total


def call_fold(v, copies):
    return pl.pallas_call(
        kernel_fold,
        out_shape=jax.ShapeDtypeStruct((copies, CHUNK, 128), BF),
        in_specs=[VMEM],
        out_specs=VMEM,
        compiler_params=params(8),
        cost_estimate=cost(10**6, 10**6),
    )(v)


def shifted(block, distance):
    devices = range(8)
    route = [(i - distance, i) for i in devices if i - distance in devices]
    return lax.ppermute(block, TM, route)


def swapped(block):
    return lax.ppermute(block, "c", [(0, 1), (1, 0)])


def exchange(value, axes):
    return lax.all_to_all(value, axes, 0, 0, tiled=True)


def shards(clips, cotangent, clip_frames, w_conv, w_down):
    frames, rows, cols = clips.shape[1:4]
    core = lax.axis_index("c").astype(jnp.int32).reshape(1)
    last = clips[0, 2:]
    before = shifted(last, 1)
    cotangent, _ = lax.optimization_barrier((cotangent, last))
    times = lax.axis_index(TM) * 2 + jnp.arange(2, dtype=jnp.int32)
    keep = (2 * times < clip_frames[0])[:, None, None, None]
    masked = jnp.where(keep, cotangent[0], jnp.zeros_like(cotangent[0]))
    masked_after = shifted(masked[:1], -1)
    taps_conv = w_conv.reshape(27, 128, 128)
    taps_down = w_down.reshape(9, 384, 256)
    wc, wa, late = call_weights(clips[0], taps_conv, taps_down)
    hg, own, other, enc, part = call_grads(
        core, clips[0], before, masked, masked_after, wc, wa, late, taps_down
    )
    own = (own.astype(F32) + swapped(other).astype(F32)).astype(BF)
    own, part = lax.optimization_barrier((own, part))
    part = shifted(part, 1)
    own = exchange(own.reshape(32, CHUNK, 128), NEAR)
    own, part = lax.optimization_barrier((own, part))
    own = call_fold(own, 4)
    own, ends = lax.optimization_barrier((own, hg[:2]))
    after = shifted(ends, -1)
    own = call_fold(exchange(own, "zh"), 32)
    own, after = lax.optimization_barrier((own, after))
    own = exchange(own, NEAR).reshape(HALF, 128)
    clip_grad, encoded = call_clip(hg, after, taps_conv, enc, part)
    own, clip_grad, encoded = lax.optimization_barrier((own, clip_grad, encoded))
    scale = 1.0 / math.sqrt(lax.axis_size(DP) * frames * lax.axis_size(TM) * rows * cols)
    begun = call_out(kernel_own, core, own, scale)
    conv_grad, down_grad = call_out(kernel_other, core, swapped(own), scale, begun)
    return (encoded[None], clip_grad[None], conv_grad.reshape(w_conv.shape), down_grad.reshape(w_down.shape))


def solution(mesh):
    fine = Mesh(mesh.devices.reshape(2, 4, 2, 2, 4, 2), DP + TM)
    parts = P(DP, TM, None, None, None)
    in_specs = (parts, parts, P(DP), P(), P())
    out_specs = (parts, parts, P(), P())
    return jax.shard_map(shards, mesh=fine, in_specs=in_specs, out_specs=out_specs, check_vma=False)
```

```python
import functools
import math

import jax
import jax.numpy as jnp
from jax import lax
from jax.experimental import pallas as pl
from jax.experimental.pallas import tpu as pltpu
from jax.sharding import Mesh
from jax.sharding import PartitionSpec as P

TM = ("y", "xh")
DP = ("xl", "zh", "zl", "c")
NEAR = ("zl", "y", "xl", "xh")

BF = jnp.bfloat16
F32 = jnp.float32
VMEM = pl.BlockSpec(memory_space=pltpu.VMEM)
SMEM = pl.BlockSpec(memory_space=pltpu.SMEM)
ANY = pl.BlockSpec(memory_space=pl.ANY)
HBM = pl.BlockSpec(memory_space=pltpu.HBM)
HALF = 42 * 128
EARLY = 7


def params(mib):
    return pltpu.CompilerParams(vmem_limit_bytes=mib * 1024 * 1024)


def cost(flops, moved):
    return pl.CostEstimate(flops=flops, bytes_accessed=moved, transcendentals=0)


def dot(a, b):
    return jnp.dot(a, b, preferred_element_type=F32)


def turned(v):
    return v.astype(F32).T.astype(BF)


def column(shape):
    return lax.broadcasted_iota(jnp.int32, shape, 1)


def from_left(v):
    return jnp.where(column(v.shape) == 0, 0.0, pltpu.roll(v, 1, 1))


def from_right(v):
    last = v.shape[1] - 1
    return jnp.where(column(v.shape) == last, 0.0, pltpu.roll(v, last, 1))


def spread(dst, frame, even, odd):
    dst[frame, 1:17, :, 0:128] = even.astype(BF)
    dst[frame, 1:17, :, 128:256] = odd.astype(BF)
    dst[frame, 1:17, :, 256:384] = from_left(odd).astype(BF)
    dst[frame, 1:17, :, 384:512] = from_right(even).astype(BF)


def split_columns(wide, v):
    wide[...] = v.astype(F32)
    return wide[:, pl.ds(0, 32, stride=2), :], wide[:, pl.ds(1, 32, stride=2), :]


def clear_edges(dst, frames):
    z = jnp.zeros((frames, 1, 32, 512), BF)
    dst[:, 0:1] = z
    dst[:, 17:18] = z


def conv_frame(frames, w_ref):
    acc = None
    for k in range(3):
        for a in range(3):
            lhs = frames[k][a : a + 16].reshape(512, 512)
            term = dot(lhs, w_ref[3 * k + a])
            acc = term if acc is None else acc + term
    return acc


def pair_weights(dst, tap, w):
    z = jnp.zeros((128, 128), BF)
    rows = ((w[1], w[0]), (w[2], w[1]), (w[0], z), (z, w[2]))
    for r, (even, odd) in enumerate(rows):
        dst[tap, 128 * r : 128 * r + 128, 0:128] = even
        dst[tap, 128 * r : 128 * r + 128, 128:256] = odd


def both_weights(wc_ref, wa_ref, wconv_ref, wd_ref):
    z = jnp.zeros((256, 128), BF)
    for tap in range(9):
        pair_weights(wc_ref, tap, [wconv_ref[3 * tap + b] for b in range(3)])
        w = [turned(wd_ref[tap, 128 * b : 128 * b + 128]) for b in range(3)]
        wa_ref[tap, 0:256, 0:128] = w[1]
        wa_ref[tap, 0:256, 128:256] = w[2]
        wa_ref[tap, 256:512, 0:128] = z
        wa_ref[tap, 256:512, 128:256] = w[0]


def up_terms(ms, t, k, wa_ref):
    here = ms[t, 0:8].reshape(256, 512)
    below = ms[t, 1:9].reshape(256, 512)
    even = dot(here, wa_ref[3 * k + 1])
    odd = dot(here, wa_ref[3 * k + 2]) + dot(below, wa_ref[3 * k])
    return even.reshape(8, 32, 256), odd.reshape(8, 32, 256)


def spread_out(ms, t, m):
    ms[t, 0:8, :, 0:256] = m
    ms[t, 0:8, :, 256:512] = from_right(m.astype(F32)).astype(BF)
    ms[t, 8:9] = jnp.zeros((1, 32, 512), BF)


def activate(hidden, acs, f):
    sig = 0.5 * jnp.tanh(0.5 * hidden) + 0.5
    act = (hidden * sig).reshape(8, 2, 32, 256)
    left = from_left(act[..., 128:256].reshape(16, 32, 128)).reshape(8, 2, 32, 128)
    actb = act.astype(BF)
    leftb = left.astype(BF)
    acs[f, 0:1, 0:1] = jnp.zeros((1, 1, 32, 384), BF)
    acs[f, 8:9, 1:2] = jnp.zeros((1, 1, 32, 384), BF)
    acs[f, 0:8, 1, :, 128:384] = actb[:, 0]
    acs[f, 1:9, 0, :, 128:384] = actb[:, 1]
    acs[f, 0:8, 1, :, 0:128] = leftb[:, 0]
    acs[f, 1:9, 0, :, 0:128] = leftb[:, 1]
    return sig * (1.0 + hidden * (1.0 - sig))


def tap_rows(acs, f, a):
    rows = (acs[f, 0:8, 0], acs[f, 0:8, 1], acs[f, 1:9, 0])[a]
    return rows.reshape(256, 384)


def encode(pairs, wd_ref):
    acc = None
    for acs, f, k in pairs:
        for a in range(3):
            term = dot(tap_rows(acs, f, a), wd_ref[3 * k + a])
            acc = term if acc is None else acc + term
    return acc.reshape(8, 32, 256)


def kernel_first(x_ref, m_ref, wconv_ref, wd_ref,
                 wc_ref, wa_ref, xs_ref, acs_ref, slope_ref, dact_ref, mt_ref, part_ref,
                 wide, ms):
    both_weights(wc_ref, wa_ref, wconv_ref, wd_ref)
    clear_edges(xs_ref, 4)
    for f in range(4):
        spread(xs_ref, f, *split_columns(wide.at[f % 2], x_ref[f]))
    for t in range(2):
        spread_out(ms, t, m_ref[t])
        mt_ref[:, 256 * t : 256 * t + 256] = turned(m_ref[t].reshape(256, 256))
    for f in range(2):
        hidden = conv_frame([xs_ref.at[f + k] for k in range(3)], wc_ref)
        slope_ref[f] = activate(hidden, acs_ref, f)
    part_ref[0] = encode(((acs_ref, 0, 0), (acs_ref, 1, 1)), wd_ref).astype(BF)
    even, odd = up_terms(ms, 0, 2, wa_ref)
    even_b, odd_b = up_terms(ms, 1, 0, wa_ref)
    dact_ref[0, :, 0] = even + even_b
    dact_ref[0, :, 1] = odd + odd_b
    for f, k in ((1, 1), (2, 2)):
        even, odd = up_terms(ms, 1, k, wa_ref)
        dact_ref[f, :, 0] = even
        dact_ref[f, :, 1] = odd


def call_first(x, m, w_conv, w_down):
    return pl.pallas_call(
        kernel_first,
        out_shape=(
            jax.ShapeDtypeStruct((9, 512, 256), BF),
            jax.ShapeDtypeStruct((9, 512, 256), BF),
            jax.ShapeDtypeStruct((4, 18, 32, 512), BF),
            jax.ShapeDtypeStruct((2, 9, 2, 32, 384), BF),
            jax.ShapeDtypeStruct((2, 512, 256), F32),
            jax.ShapeDtypeStruct((3, 8, 2, 32, 256), F32),
            jax.ShapeDtypeStruct((256, 512), BF),
            jax.ShapeDtypeStruct((1, 8, 32, 256), BF),
        ),
        in_specs=[VMEM] * 4,
        out_specs=(VMEM,) * 8,
        scratch_shapes=[
            pltpu.VMEM((2, 16, 64, 128), F32),
            pltpu.VMEM((2, 9, 32, 512), BF),
        ],
        compiler_params=params(12),
        cost_estimate=cost(10**6, 10**6),
    )(x, m, w_conv, w_down)


def kernel_grads(core_ref, before_ref, next_ref, wc_ref, wa_ref, wd_ref, xs_ref, high_ref, slope_ref, dact_ref, mt_ref,
                 hg_ref, own_ref, other_ref, even_ref, odd_ref,
                 wide, ms, up, hgt, low, xb, mn, sums, sems):
    core = core_ref[0]
    sums[0, HALF - 128 :] = jnp.zeros((128, 128), BF)
    sums[1, HALF - 256 :] = jnp.zeros((256, 128), BF)
    clear_edges(xb, 2)
    for f in range(2):
        spread(xb, f, *split_columns(wide.at[f], before_ref[f]))
    spread_out(ms, 0, next_ref[0])
    mn[...] = turned(next_ref[0].reshape(256, 256))
    for k in range(2):
        even, odd = up_terms(ms, 0, k, wa_ref)
        up[k, :, 0] = even
        up[k, :, 1] = odd
    every = [xb.at[f] for f in range(2)] + [xs_ref.at[f] for f in range(2)]
    for f in (2, 3, 0, 1):
        if f < 2:
            slope = activate(conv_frame(every[f : f + 3], wc_ref), low, f)
            grad = dact_ref[f].reshape(512, 256) * slope
        elif f == 2:
            grad = (dact_ref[2] + up[0]).reshape(512, 256) * slope_ref[0]
        else:
            grad = up[1].reshape(512, 256) * slope_ref[1]
        hg_ref[f] = grad.astype(BF).reshape(16, 32, 256)
        hgt[:, 512 * f : 512 * f + 512] = grad.T.astype(BF)

    def put(half, block, v):
        sums[half, 128 * block : 128 * block + 128] = v

    for k in range(3):
        left = mt_ref[...] if k == 2 else jnp.concatenate([mt_ref[:, 256:512], mn[...]], axis=1)
        f = 1 if k == 1 else 0
        for a in range(3):
            right = jnp.concatenate([tap_rows(low, f, a), tap_rows(high_ref, f, a)], axis=0)
            g = dot(left, right)
            for b in range(3):
                block = g[:, 128 * b : 128 * b + 128].T.astype(BF)
                at = 9 * k + 3 * a + b
                half, first = (0, 27 + 2 * at) if at < EARLY else (1, 2 * (at - EARLY))
                put(half, first, block[:, 0:128])
                put(half, first + 1, block[:, 128:256])

    for k in range(3):
        for a in range(3):
            right = xs_ref[0 : k + 2, a : a + 16].reshape(512 * (k + 2), 512)
            if k < 2:
                first = xb[k:2, a : a + 16].reshape(512 * (2 - k), 512)
                right = jnp.concatenate([first, right], axis=0)
            g = dot(hgt[...], right)
            for b in range(3):
                u, v = (2, 0, 1)[b], (0, 1, 3)[b]
                both = g[0:128, 128 * u : 128 * u + 128] + g[128:256, 128 * v : 128 * v + 128]
                put(0, 9 * k + 3 * a + b, both.T.astype(BF))

    send = pltpu.make_async_copy(sums.at[1 - core], other_ref, sems.at[0])
    keep = pltpu.make_async_copy(sums.at[core], own_ref, sems.at[1])
    send.start()
    keep.start()
    even_ref[...] = encode(((low, 0, 2),), wd_ref)
    pairs = ((low, 0, 0), (low, 1, 1), (high_ref, 0, 2))
    odd_ref[...] = encode(pairs, wd_ref).astype(BF)
    send.wait()
    keep.wait()


def call_grads(core, before, after, wc, wa, wd, xs, high, slope, dact, mt):
    return pl.pallas_call(
        kernel_grads,
        out_shape=(
            jax.ShapeDtypeStruct((4, 16, 32, 256), BF),
            jax.ShapeDtypeStruct((HALF, 128), BF),
            jax.ShapeDtypeStruct((HALF, 128), BF),
            jax.ShapeDtypeStruct((8, 32, 256), F32),
            jax.ShapeDtypeStruct((8, 32, 256), BF),
        ),
        in_specs=[SMEM] + [VMEM] * 10,
        out_specs=(VMEM, ANY, ANY, VMEM, VMEM),
        scratch_shapes=[
            pltpu.VMEM((2, 16, 64, 128), F32),
            pltpu.VMEM((1, 9, 32, 512), BF),
            pltpu.VMEM((2, 8, 2, 32, 256), F32),
            pltpu.VMEM((256, 2048), BF),
            pltpu.VMEM((2, 9, 2, 32, 384), BF),
            pltpu.VMEM((2, 18, 32, 512), BF),
            pltpu.VMEM((256, 256), BF),
            pltpu.VMEM((2, HALF, 128), BF),
            pltpu.SemaphoreType.DMA((2,)),
        ],
        compiler_params=params(24),
        cost_estimate=cost(10**6, 10**6),
    )(core, before, after, wc, wa, wd, xs, high, slope, dact, mt)


def kernel_clip(h_ref, after_ref, w_ref, even_ref, odd_ref, part_ref,
                out_ref, enc_ref, hs, wt, wide):
    enc_ref[0] = (even_ref[...] + part_ref[0].astype(F32)).astype(BF)
    enc_ref[1] = odd_ref[...]
    clear_edges(hs, 6)
    for tap in range(9):
        pair_weights(wt, tap, [turned(w_ref[3 * (8 - tap) + 2 - b]) for b in range(3)])
    for f in range(6):
        v = (h_ref[f] if f < 4 else after_ref[f - 4]).astype(F32)
        spread(hs, f, v[:, :, 0:128], v[:, :, 128:256])
    for f in range(4):
        v = conv_frame([hs.at[f + k] for k in range(3)], wt).reshape(16, 32, 256)
        wide[f % 2, :, pl.ds(0, 32, stride=2), :] = v[:, :, 0:128]
        wide[f % 2, :, pl.ds(1, 32, stride=2), :] = v[:, :, 128:256]
        out_ref[f] = wide[f % 2].astype(BF)


def call_clip(h, after, w, even, odd, part):
    return pl.pallas_call(
        kernel_clip,
        out_shape=(
            jax.ShapeDtypeStruct((4, 16, 64, 128), BF),
            jax.ShapeDtypeStruct((2, 8, 32, 256), BF),
        ),
        in_specs=[VMEM] * 6,
        out_specs=(VMEM, VMEM),
        scratch_shapes=[
            pltpu.VMEM((6, 18, 32, 512), BF),
            pltpu.VMEM((9, 512, 256), BF),
            pltpu.VMEM((2, 16, 64, 128), F32),
        ],
        compiler_params=params(32),
        cost_estimate=cost(5 * 10**9, 5 * 10**6),
    )(h, after, w, even, odd, part)


def write_half(half, scale, src, conv_ref, down_ref, conv, down, sems):
    def block(at):
        return src[128 * at : 128 * at + 128].astype(F32) * scale

    @pl.when(half == 0)
    def _():
        for at in range(27):
            conv[at] = block(at)
        to_conv = pltpu.make_async_copy(conv, conv_ref, sems.at[0])
        to_conv.start()
        for at in range(EARLY):
            down[at, :, 0:128] = block(27 + 2 * at)
            down[at, :, 128:256] = block(28 + 2 * at)
        to_down = pltpu.make_async_copy(down.at[0:EARLY], down_ref.at[0:EARLY], sems.at[1])
        to_down.start()
        to_conv.wait()
        to_down.wait()

    @pl.when(half == 1)
    def _():
        pieces = ((0, 7), (7, 14), (14, 27 - EARLY))
        copies = []
        for i, (first, last) in enumerate(pieces):
            for at in range(first, last):
                down[at, :, 0:128] = block(2 * at)
                down[at, :, 128:256] = block(2 * at + 1)
            target = down_ref.at[EARLY + first : EARLY + last]
            copies.append(pltpu.make_async_copy(down.at[first:last], target, sems.at[i]))
            copies[-1].start()
        for copy in copies:
            copy.wait()


def kernel_own(scale, core_ref, src, conv_ref, down_ref, conv, down, sems):
    write_half(core_ref[0], scale, src, conv_ref, down_ref, conv, down, sems)


def kernel_other(scale, core_ref, src, conv_in, down_in, conv_ref, down_ref, conv, down, sems):
    write_half(1 - core_ref[0], scale, src, conv_ref, down_ref, conv, down, sems)


def call_out(kernel, core, half, scale, begun=()):
    return pl.pallas_call(
        functools.partial(kernel, scale),
        out_shape=(pltpu.HBM((27, 128, 128), F32), pltpu.HBM((27, 128, 256), F32)),
        in_specs=[SMEM, VMEM] + [HBM] * len(begun),
        out_specs=(HBM, HBM),
        input_output_aliases={2: 0, 3: 1} if begun else {},
        scratch_shapes=[
            pltpu.VMEM((27, 128, 128), F32),
            pltpu.VMEM((27 - EARLY, 128, 256), F32),
            pltpu.SemaphoreType.DMA((3,)),
        ],
        compiler_params=params(16),
        cost_estimate=cost(10**6, 4 * 10**6),
    )(core, half, *begun)


CHUNK = HALF // 32


def kernel_fold(in_ref, out_ref):
    total = in_ref[0].astype(F32)
    for i in range(1, in_ref.shape[0]):
        total += in_ref[i].astype(F32)
    total = total.astype(BF)
    for i in range(out_ref.shape[0]):
        out_ref[i] = total


def call_fold(v, copies):
    return pl.pallas_call(
        kernel_fold,
        out_shape=jax.ShapeDtypeStruct((copies, CHUNK, 128), BF),
        in_specs=[VMEM],
        out_specs=VMEM,
        compiler_params=params(8),
        cost_estimate=cost(10**6, 10**6),
    )(v)


def shifted(block, distance):
    devices = range(8)
    route = [(i - distance, i) for i in devices if i - distance in devices]
    return lax.ppermute(block, TM, route)


def swapped(block):
    return lax.ppermute(block, "c", [(0, 1), (1, 0)])


def exchange(value, axes):
    return lax.all_to_all(value, axes, 0, 0, tiled=True)


def shards(clips, cotangent, clip_frames, w_conv, w_down):
    frames, rows, cols = clips.shape[1:4]
    core = lax.axis_index("c").astype(jnp.int32).reshape(1)
    last = clips[0, 2:]
    before = shifted(last, 1)
    cotangent, _ = lax.optimization_barrier((cotangent, last))
    times = lax.axis_index(TM) * 2 + jnp.arange(2, dtype=jnp.int32)
    keep = (2 * times < clip_frames[0])[:, None, None, None]
    masked = jnp.where(keep, cotangent[0], jnp.zeros_like(cotangent[0]))
    masked_after = shifted(masked[:1], -1)
    taps_conv = w_conv.reshape(27, 128, 128)
    taps_down = w_down.reshape(9, 384, 256)
    wc, wa, xs, high, slope, dact, mt, part = call_first(clips[0], masked, taps_conv, taps_down)
    hg, own, other, even, odd = call_grads(
        core, before, masked_after, wc, wa, taps_down, xs, high, slope, dact, mt
    )
    own = (own.astype(F32) + swapped(other).astype(F32)).astype(BF)
    own, part = lax.optimization_barrier((own, part))
    part = shifted(part, 1)
    own = exchange(own.reshape(32, CHUNK, 128), NEAR)
    own, part = lax.optimization_barrier((own, part))
    own = call_fold(own, 4)
    own, ends = lax.optimization_barrier((own, hg[:2]))
    after = shifted(ends, -1)
    own = call_fold(exchange(own, "zh"), 32)
    own, after = lax.optimization_barrier((own, after))
    own = exchange(own, NEAR).reshape(HALF, 128)
    clip_grad, encoded = call_clip(hg, after, taps_conv, even, odd, part)
    own, clip_grad, encoded = lax.optimization_barrier((own, clip_grad, encoded))
    scale = 1.0 / math.sqrt(lax.axis_size(DP) * frames * lax.axis_size(TM) * rows * cols)
    begun = call_out(kernel_own, core, own, scale)
    conv_grad, down_grad = call_out(kernel_other, core, swapped(own), scale, begun)
    return (encoded[None], clip_grad[None], conv_grad.reshape(w_conv.shape), down_grad.reshape(w_down.shape))


def solution(mesh):
    fine = Mesh(mesh.devices.reshape(2, 4, 2, 2, 4, 2), DP + TM)
    parts = P(DP, TM, None, None, None)
    in_specs = (parts, parts, P(DP), P(), P())
    out_specs = (parts, parts, P(), P())
    return jax.shard_map(shards, mesh=fine, in_specs=in_specs, out_specs=out_specs, check_vma=False)
```

```python
import functools
import math

import jax
import jax.numpy as jnp
from jax import lax
from jax.experimental import pallas as pl
from jax.experimental.pallas import tpu as pltpu
from jax.sharding import Mesh
from jax.sharding import PartitionSpec as P

TM = ("y", "xh")
DP = ("xl", "zh", "zl", "c")
NEAR = ("zl", "y", "xl", "xh")

BF = jnp.bfloat16
F32 = jnp.float32
VMEM = pl.BlockSpec(memory_space=pltpu.VMEM)
SMEM = pl.BlockSpec(memory_space=pltpu.SMEM)
ANY = pl.BlockSpec(memory_space=pl.ANY)
HBM = pl.BlockSpec(memory_space=pltpu.HBM)
HALF = 44 * 128
EARLY = 7


def params(mib):
    return pltpu.CompilerParams(vmem_limit_bytes=mib * 1024 * 1024)


def cost(flops, moved):
    return pl.CostEstimate(flops=flops, bytes_accessed=moved, transcendentals=0)


def dot(a, b):
    return jnp.dot(a, b, preferred_element_type=F32)


def turned(v):
    return v.astype(F32).T.astype(BF)


def column(shape):
    return lax.broadcasted_iota(jnp.int32, shape, 1)


def from_left(v):
    return jnp.where(column(v.shape) == 0, 0.0, pltpu.roll(v, 1, 1))


def from_right(v):
    last = v.shape[1] - 1
    return jnp.where(column(v.shape) == last, 0.0, pltpu.roll(v, last, 1))


def spread(dst, frame, even, odd):
    dst[frame, 1:17, :, 0:128] = even.astype(BF)
    dst[frame, 1:17, :, 128:256] = odd.astype(BF)
    dst[frame, 1:17, :, 256:384] = from_left(odd).astype(BF)
    dst[frame, 1:17, :, 384:512] = from_right(even).astype(BF)


def split_columns(wide, v):
    wide[...] = v.astype(F32)
    return wide[:, pl.ds(0, 32, stride=2), :], wide[:, pl.ds(1, 32, stride=2), :]


def clear_edges(dst, frames):
    z = jnp.zeros((frames, 1, 32, 512), BF)
    dst[:, 0:1] = z
    dst[:, 17:18] = z


def conv_frame(frames, w_ref):
    acc = None
    for k in range(3):
        for a in range(3):
            lhs = frames[k][a : a + 16].reshape(512, 512)
            term = dot(lhs, w_ref[3 * k + a])
            acc = term if acc is None else acc + term
    return acc


def pair_weights(dst, tap, w):
    z = jnp.zeros((128, 128), BF)
    rows = ((w[1], w[0]), (w[2], w[1]), (w[0], z), (z, w[2]))
    for r, (even, odd) in enumerate(rows):
        dst[tap, 128 * r : 128 * r + 128, 0:128] = even
        dst[tap, 128 * r : 128 * r + 128, 128:256] = odd


def both_weights(wc_ref, wa_ref, wconv_ref, wd_ref):
    z = jnp.zeros((256, 128), BF)
    for tap in range(9):
        pair_weights(wc_ref, tap, [wconv_ref[3 * tap + b] for b in range(3)])
        w = [turned(wd_ref[tap, 128 * b : 128 * b + 128]) for b in range(3)]
        wa_ref[tap, 0:256, 0:128] = w[1]
        wa_ref[tap, 0:256, 128:256] = w[2]
        wa_ref[tap, 256:512, 0:128] = z
        wa_ref[tap, 256:512, 128:256] = w[0]


def up_terms(ms, t, k, wa_ref):
    here = ms[t, 0:8].reshape(256, 512)
    below = ms[t, 1:9].reshape(256, 512)
    even = dot(here, wa_ref[3 * k + 1])
    odd = dot(here, wa_ref[3 * k + 2]) + dot(below, wa_ref[3 * k])
    return even.reshape(8, 32, 256), odd.reshape(8, 32, 256)


def spread_out(ms, t, m):
    ms[t, 0:8, :, 0:256] = m
    ms[t, 0:8, :, 256:512] = from_right(m.astype(F32)).astype(BF)
    ms[t, 8:9] = jnp.zeros((1, 32, 512), BF)


def activate(hidden, acs, f):
    sig = 0.5 * jnp.tanh(0.5 * hidden) + 0.5
    act = (hidden * sig).reshape(8, 2, 32, 256)
    left = from_left(act[..., 128:256].reshape(16, 32, 128)).reshape(8, 2, 32, 128)
    actb = act.astype(BF)
    leftb = left.astype(BF)
    acs[f, 0:1, 0:1] = jnp.zeros((1, 1, 32, 384), BF)
    acs[f, 8:9, 1:2] = jnp.zeros((1, 1, 32, 384), BF)
    acs[f, 0:8, 1, :, 128:384] = actb[:, 0]
    acs[f, 1:9, 0, :, 128:384] = actb[:, 1]
    acs[f, 0:8, 1, :, 0:128] = leftb[:, 0]
    acs[f, 1:9, 0, :, 0:128] = leftb[:, 1]
    return sig * (1.0 + hidden * (1.0 - sig))


def tap_rows(acs, f, a):
    rows = (acs[f, 0:8, 0], acs[f, 0:8, 1], acs[f, 1:9, 0])[a]
    return rows.reshape(256, 384)


def encode(pairs, wd_ref):
    acc = None
    for acs, f, k in pairs:
        for a in range(3):
            term = dot(tap_rows(acs, f, a), wd_ref[3 * k + a])
            acc = term if acc is None else acc + term
    return acc.reshape(8, 32, 256)


def kernel_first(x_ref, m_ref, wconv_ref, wd_ref,
                 wc_ref, wa_ref, xs_ref, acs_ref, slope_ref, dact_ref, mt_ref, part_ref,
                 wide, ms):
    both_weights(wc_ref, wa_ref, wconv_ref, wd_ref)
    clear_edges(xs_ref, 4)
    for f in range(4):
        spread(xs_ref, f, *split_columns(wide.at[f % 2], x_ref[f]))
    for t in range(2):
        spread_out(ms, t, m_ref[t])
        mt_ref[:, 256 * t : 256 * t + 256] = turned(m_ref[t].reshape(256, 256))
    for f in range(2):
        hidden = conv_frame([xs_ref.at[f + k] for k in range(3)], wc_ref)
        slope_ref[f] = activate(hidden, acs_ref, f)
    part_ref[0] = encode(((acs_ref, 0, 0), (acs_ref, 1, 1)), wd_ref).astype(BF)
    even, odd = up_terms(ms, 0, 2, wa_ref)
    even_b, odd_b = up_terms(ms, 1, 0, wa_ref)
    dact_ref[0, :, 0] = even + even_b
    dact_ref[0, :, 1] = odd + odd_b
    for f, k in ((1, 1), (2, 2)):
        even, odd = up_terms(ms, 1, k, wa_ref)
        dact_ref[f, :, 0] = even
        dact_ref[f, :, 1] = odd


def call_first(x, m, w_conv, w_down):
    return pl.pallas_call(
        kernel_first,
        out_shape=(
            jax.ShapeDtypeStruct((9, 512, 256), BF),
            jax.ShapeDtypeStruct((9, 512, 256), BF),
            jax.ShapeDtypeStruct((4, 18, 32, 512), BF),
            jax.ShapeDtypeStruct((2, 9, 2, 32, 384), BF),
            jax.ShapeDtypeStruct((2, 512, 256), F32),
            jax.ShapeDtypeStruct((3, 8, 2, 32, 256), F32),
            jax.ShapeDtypeStruct((256, 512), BF),
            jax.ShapeDtypeStruct((1, 8, 32, 256), BF),
        ),
        in_specs=[VMEM] * 4,
        out_specs=(VMEM,) * 8,
        scratch_shapes=[
            pltpu.VMEM((2, 16, 64, 128), F32),
            pltpu.VMEM((2, 9, 32, 512), BF),
        ],
        compiler_params=params(12),
        cost_estimate=cost(10**6, 10**6),
    )(x, m, w_conv, w_down)


def kernel_grads(core_ref, before_ref, next_ref, wc_ref, wa_ref, wd_ref, xs_ref, high_ref, slope_ref, dact_ref, mt_ref,
                 hg_ref, own_ref, other_ref, even_ref, odd_ref,
                 wide, ms, up, hgt, low, xb, mn, sums, sems):
    core = core_ref[0]
    sums[0, 41 * 128 :] = jnp.zeros((HALF - 41 * 128, 128), BF)
    sums[1, 40 * 128 :] = jnp.zeros((HALF - 40 * 128, 128), BF)
    clear_edges(xb, 2)
    for f in range(2):
        spread(xb, f, *split_columns(wide.at[f], before_ref[f]))
    spread_out(ms, 0, next_ref[0])
    mn[...] = turned(next_ref[0].reshape(256, 256))
    for k in range(2):
        even, odd = up_terms(ms, 0, k, wa_ref)
        up[k, :, 0] = even
        up[k, :, 1] = odd
    every = [xb.at[f] for f in range(2)] + [xs_ref.at[f] for f in range(2)]
    for f in (2, 3, 0, 1):
        if f < 2:
            slope = activate(conv_frame(every[f : f + 3], wc_ref), low, f)
            grad = dact_ref[f].reshape(512, 256) * slope
        elif f == 2:
            grad = (dact_ref[2] + up[0]).reshape(512, 256) * slope_ref[0]
        else:
            grad = up[1].reshape(512, 256) * slope_ref[1]
        hg_ref[f] = grad.astype(BF).reshape(16, 32, 256)
        hgt[:, 512 * f : 512 * f + 512] = grad.T.astype(BF)

    def put(half, block, v):
        sums[half, 128 * block : 128 * block + 128] = v

    for k in range(3):
        left = mt_ref[...] if k == 2 else jnp.concatenate([mt_ref[:, 256:512], mn[...]], axis=1)
        f = 1 if k == 1 else 0
        for a in range(3):
            right = jnp.concatenate([tap_rows(low, f, a), tap_rows(high_ref, f, a)], axis=0)
            g = dot(left, right)
            for b in range(3):
                block = g[:, 128 * b : 128 * b + 128].T.astype(BF)
                at = 9 * k + 3 * a + b
                half, first = (0, 27 + 2 * at) if at < EARLY else (1, 2 * (at - EARLY))
                put(half, first, block[:, 0:128])
                put(half, first + 1, block[:, 128:256])

    for k in range(3):
        for a in range(3):
            right = xs_ref[0 : k + 2, a : a + 16].reshape(512 * (k + 2), 512)
            if k < 2:
                first = xb[k:2, a : a + 16].reshape(512 * (2 - k), 512)
                right = jnp.concatenate([first, right], axis=0)
            g = dot(hgt[...], right)
            for b in range(3):
                u, v = (2, 0, 1)[b], (0, 1, 3)[b]
                both = g[0:128, 128 * u : 128 * u + 128] + g[128:256, 128 * v : 128 * v + 128]
                put(0, 9 * k + 3 * a + b, both.T.astype(BF))

    send = pltpu.make_async_copy(sums.at[1 - core], other_ref, sems.at[0])
    keep = pltpu.make_async_copy(sums.at[core], own_ref, sems.at[1])
    send.start()
    keep.start()
    even_ref[...] = encode(((low, 0, 2),), wd_ref)
    pairs = ((low, 0, 0), (low, 1, 1), (high_ref, 0, 2))
    odd_ref[...] = encode(pairs, wd_ref).astype(BF)
    send.wait()
    keep.wait()


def call_grads(core, before, after, wc, wa, wd, xs, high, slope, dact, mt):
    return pl.pallas_call(
        kernel_grads,
        out_shape=(
            jax.ShapeDtypeStruct((4, 16, 32, 256), BF),
            jax.ShapeDtypeStruct((HALF, 128), BF),
            jax.ShapeDtypeStruct((HALF, 128), BF),
            jax.ShapeDtypeStruct((8, 32, 256), F32),
            jax.ShapeDtypeStruct((8, 32, 256), BF),
        ),
        in_specs=[SMEM] + [VMEM] * 10,
        out_specs=(VMEM, ANY, ANY, VMEM, VMEM),
        scratch_shapes=[
            pltpu.VMEM((2, 16, 64, 128), F32),
            pltpu.VMEM((1, 9, 32, 512), BF),
            pltpu.VMEM((2, 8, 2, 32, 256), F32),
            pltpu.VMEM((256, 2048), BF),
            pltpu.VMEM((2, 9, 2, 32, 384), BF),
            pltpu.VMEM((2, 18, 32, 512), BF),
            pltpu.VMEM((256, 256), BF),
            pltpu.VMEM((2, HALF, 128), BF),
            pltpu.SemaphoreType.DMA((2,)),
        ],
        compiler_params=params(24),
        cost_estimate=cost(10**6, 10**6),
    )(core, before, after, wc, wa, wd, xs, high, slope, dact, mt)


def kernel_clip(h_ref, after_ref, w_ref, even_ref, odd_ref, part_ref,
                out_ref, enc_ref, hs, wt, wide):
    enc_ref[0] = (even_ref[...] + part_ref[0].astype(F32)).astype(BF)
    enc_ref[1] = odd_ref[...]
    clear_edges(hs, 6)
    for tap in range(9):
        pair_weights(wt, tap, [turned(w_ref[3 * (8 - tap) + 2 - b]) for b in range(3)])
    for f in range(6):
        v = (h_ref[f] if f < 4 else after_ref[f - 4]).astype(F32)
        spread(hs, f, v[:, :, 0:128], v[:, :, 128:256])
    for f in range(4):
        v = conv_frame([hs.at[f + k] for k in range(3)], wt).reshape(16, 32, 256)
        wide[f % 2, :, pl.ds(0, 32, stride=2), :] = v[:, :, 0:128]
        wide[f % 2, :, pl.ds(1, 32, stride=2), :] = v[:, :, 128:256]
        out_ref[f] = wide[f % 2].astype(BF)


def call_clip(h, after, w, even, odd, part):
    return pl.pallas_call(
        kernel_clip,
        out_shape=(
            jax.ShapeDtypeStruct((4, 16, 64, 128), BF),
            jax.ShapeDtypeStruct((2, 8, 32, 256), BF),
        ),
        in_specs=[VMEM] * 6,
        out_specs=(VMEM, VMEM),
        scratch_shapes=[
            pltpu.VMEM((6, 18, 32, 512), BF),
            pltpu.VMEM((9, 512, 256), BF),
            pltpu.VMEM((2, 16, 64, 128), F32),
        ],
        compiler_params=params(32),
        cost_estimate=cost(5 * 10**9, 5 * 10**6),
    )(h, after, w, even, odd, part)


def write_half(half, scale, src, conv_ref, down_ref, conv, down, sems):
    def block(at):
        return src[128 * at : 128 * at + 128].astype(F32) * scale

    @pl.when(half == 0)
    def _():
        for at in range(27):
            conv[at] = block(at)
        to_conv = pltpu.make_async_copy(conv, conv_ref, sems.at[0])
        to_conv.start()
        for at in range(EARLY):
            down[at, :, 0:128] = block(27 + 2 * at)
            down[at, :, 128:256] = block(28 + 2 * at)
        to_down = pltpu.make_async_copy(down.at[0:EARLY], down_ref.at[0:EARLY], sems.at[1])
        to_down.start()
        to_conv.wait()
        to_down.wait()

    @pl.when(half == 1)
    def _():
        pieces = ((0, 7), (7, 14), (14, 27 - EARLY))
        copies = []
        for i, (first, last) in enumerate(pieces):
            for at in range(first, last):
                down[at, :, 0:128] = block(2 * at)
                down[at, :, 128:256] = block(2 * at + 1)
            target = down_ref.at[EARLY + first : EARLY + last]
            copies.append(pltpu.make_async_copy(down.at[first:last], target, sems.at[i]))
            copies[-1].start()
        for copy in copies:
            copy.wait()


def kernel_own(scale, core_ref, src, conv_ref, down_ref, conv, down, sems):
    write_half(core_ref[0], scale, src, conv_ref, down_ref, conv, down, sems)


def kernel_other(scale, core_ref, src, conv_in, down_in, conv_ref, down_ref, conv, down, sems):
    write_half(1 - core_ref[0], scale, src, conv_ref, down_ref, conv, down, sems)


def call_out(kernel, core, half, scale, begun=()):
    return pl.pallas_call(
        functools.partial(kernel, scale),
        out_shape=(pltpu.HBM((27, 128, 128), F32), pltpu.HBM((27, 128, 256), F32)),
        in_specs=[SMEM, VMEM] + [HBM] * len(begun),
        out_specs=(HBM, HBM),
        input_output_aliases={2: 0, 3: 1} if begun else {},
        scratch_shapes=[
            pltpu.VMEM((27, 128, 128), F32),
            pltpu.VMEM((27 - EARLY, 128, 256), F32),
            pltpu.SemaphoreType.DMA((3,)),
        ],
        compiler_params=params(16),
        cost_estimate=cost(10**6, 4 * 10**6),
    )(core, half, *begun)


CHUNK = HALF // 32


def kernel_fold(in_ref, out_ref):
    total = in_ref[0].astype(F32)
    for i in range(1, in_ref.shape[0]):
        total += in_ref[i].astype(F32)
    total = total.astype(BF)
    for i in range(out_ref.shape[0]):
        out_ref[i] = total


def call_fold(v, copies):
    return pl.pallas_call(
        kernel_fold,
        out_shape=jax.ShapeDtypeStruct((copies, CHUNK, 128), BF),
        in_specs=[VMEM],
        out_specs=VMEM,
        compiler_params=params(8),
        cost_estimate=cost(10**6, 10**6),
    )(v)


def shifted(block, distance):
    devices = range(8)
    route = [(i - distance, i) for i in devices if i - distance in devices]
    return lax.ppermute(block, TM, route)


def swapped(block):
    return lax.ppermute(block, "c", [(0, 1), (1, 0)])


def exchange(value, axes):
    return lax.all_to_all(value, axes, 0, 0, tiled=True)


def shards(clips, cotangent, clip_frames, w_conv, w_down):
    frames, rows, cols = clips.shape[1:4]
    core = lax.axis_index("c").astype(jnp.int32).reshape(1)
    last = clips[0, 2:]
    before = shifted(last, 1)
    cotangent, _ = lax.optimization_barrier((cotangent, last))
    times = lax.axis_index(TM) * 2 + jnp.arange(2, dtype=jnp.int32)
    keep = (2 * times < clip_frames[0])[:, None, None, None]
    masked = jnp.where(keep, cotangent[0], jnp.zeros_like(cotangent[0]))
    masked_after = shifted(masked[:1], -1)
    taps_conv = w_conv.reshape(27, 128, 128)
    taps_down = w_down.reshape(9, 384, 256)
    wc, wa, xs, high, slope, dact, mt, part = call_first(clips[0], masked, taps_conv, taps_down)
    hg, own, other, even, odd = call_grads(
        core, before, masked_after, wc, wa, taps_down, xs, high, slope, dact, mt
    )
    own = (own.astype(F32) + swapped(other).astype(F32)).astype(BF)
    own, part = lax.optimization_barrier((own, part))
    part = shifted(part, 1)
    own = exchange(own.reshape(32, CHUNK, 128), NEAR)
    own, part = lax.optimization_barrier((own, part))
    own = call_fold(own, 4)
    own, ends = lax.optimization_barrier((own, hg[:2]))
    after = shifted(ends, -1)
    own = call_fold(exchange(own, "zh"), 32)
    own, after = lax.optimization_barrier((own, after))
    own = exchange(own, NEAR).reshape(HALF, 128)
    clip_grad, encoded = call_clip(hg, after, taps_conv, even, odd, part)
    own, clip_grad, encoded = lax.optimization_barrier((own, clip_grad, encoded))
    scale = 1.0 / math.sqrt(lax.axis_size(DP) * frames * lax.axis_size(TM) * rows * cols)
    begun = call_out(kernel_own, core, own, scale)
    conv_grad, down_grad = call_out(kernel_other, core, swapped(own), scale, begun)
    return (encoded[None], clip_grad[None], conv_grad.reshape(w_conv.shape), down_grad.reshape(w_down.shape))


def solution(mesh):
    fine = Mesh(mesh.devices.reshape(2, 4, 2, 2, 4, 2), DP + TM)
    parts = P(DP, TM, None, None, None)
    in_specs = (parts, parts, P(DP), P(), P())
    out_specs = (parts, parts, P(), P())
    return jax.shard_map(shards, mesh=fine, in_specs=in_specs, out_specs=out_specs, check_vma=False)
```

```python
import functools
import math

import jax
import jax.numpy as jnp
from jax import lax
from jax.experimental import pallas as pl
from jax.experimental.pallas import tpu as pltpu
from jax.sharding import Mesh
from jax.sharding import PartitionSpec as P

TM = ("y", "xh")
DP = ("xl", "zh", "zl", "c")
NEAR = ("zl", "xl", "xh", "y")

BF = jnp.bfloat16
F32 = jnp.float32
VMEM = pl.BlockSpec(memory_space=pltpu.VMEM)
SMEM = pl.BlockSpec(memory_space=pltpu.SMEM)
ANY = pl.BlockSpec(memory_space=pl.ANY)
HBM = pl.BlockSpec(memory_space=pltpu.HBM)
HALF = 42 * 128
EARLY = 7


def params(mib):
    return pltpu.CompilerParams(vmem_limit_bytes=mib * 1024 * 1024)


def cost(flops, moved):
    return pl.CostEstimate(flops=flops, bytes_accessed=moved, transcendentals=0)


def dot(a, b):
    return jnp.dot(a, b, preferred_element_type=F32)


def turned(v):
    return v.astype(F32).T.astype(BF)


def column(shape):
    return lax.broadcasted_iota(jnp.int32, shape, 1)


def from_left(v):
    return jnp.where(column(v.shape) == 0, 0.0, pltpu.roll(v, 1, 1))


def from_right(v):
    last = v.shape[1] - 1
    return jnp.where(column(v.shape) == last, 0.0, pltpu.roll(v, last, 1))


def spread(dst, frame, even, odd):
    dst[frame, 1:17, :, 0:128] = even.astype(BF)
    dst[frame, 1:17, :, 128:256] = odd.astype(BF)
    dst[frame, 1:17, :, 256:384] = from_left(odd).astype(BF)
    dst[frame, 1:17, :, 384:512] = from_right(even).astype(BF)


def split_columns(wide, v):
    wide[...] = v.astype(F32)
    return wide[:, pl.ds(0, 32, stride=2), :], wide[:, pl.ds(1, 32, stride=2), :]


def clear_edges(dst, frames):
    z = jnp.zeros((frames, 1, 32, 512), BF)
    dst[:, 0:1] = z
    dst[:, 17:18] = z


def conv_frame(frames, w_ref):
    acc = None
    for k in range(3):
        for a in range(3):
            lhs = frames[k][a : a + 16].reshape(512, 512)
            term = dot(lhs, w_ref[3 * k + a])
            acc = term if acc is None else acc + term
    return acc


def pair_weights(dst, tap, w):
    z = jnp.zeros((128, 128), BF)
    rows = ((w[1], w[0]), (w[2], w[1]), (w[0], z), (z, w[2]))
    for r, (even, odd) in enumerate(rows):
        dst[tap, 128 * r : 128 * r + 128, 0:128] = even
        dst[tap, 128 * r : 128 * r + 128, 128:256] = odd


def both_weights(wc_ref, wa_ref, wconv_ref, wd_ref):
    z = jnp.zeros((256, 128), BF)
    for tap in range(9):
        pair_weights(wc_ref, tap, [wconv_ref[3 * tap + b] for b in range(3)])
        w = [turned(wd_ref[tap, 128 * b : 128 * b + 128]) for b in range(3)]
        wa_ref[tap, 0:256, 0:128] = w[1]
        wa_ref[tap, 0:256, 128:256] = w[2]
        wa_ref[tap, 256:512, 0:128] = z
        wa_ref[tap, 256:512, 128:256] = w[0]


def up_terms(ms, t, k, wa_ref):
    here = ms[t, 0:8].reshape(256, 512)
    below = ms[t, 1:9].reshape(256, 512)
    even = dot(here, wa_ref[3 * k + 1])
    odd = dot(here, wa_ref[3 * k + 2]) + dot(below, wa_ref[3 * k])
    return even.reshape(8, 32, 256), odd.reshape(8, 32, 256)


def spread_out(ms, t, m):
    ms[t, 0:8, :, 0:256] = m
    ms[t, 0:8, :, 256:512] = from_right(m.astype(F32)).astype(BF)
    ms[t, 8:9] = jnp.zeros((1, 32, 512), BF)


def activate(hidden, acs, f):
    sig = 0.5 * jnp.tanh(0.5 * hidden) + 0.5
    act = (hidden * sig).reshape(8, 2, 32, 256)
    left = from_left(act[..., 128:256].reshape(16, 32, 128)).reshape(8, 2, 32, 128)
    actb = act.astype(BF)
    leftb = left.astype(BF)
    acs[f, 0:1, 0:1] = jnp.zeros((1, 1, 32, 384), BF)
    acs[f, 8:9, 1:2] = jnp.zeros((1, 1, 32, 384), BF)
    acs[f, 0:8, 1, :, 128:384] = actb[:, 0]
    acs[f, 1:9, 0, :, 128:384] = actb[:, 1]
    acs[f, 0:8, 1, :, 0:128] = leftb[:, 0]
    acs[f, 1:9, 0, :, 0:128] = leftb[:, 1]
    return sig * (1.0 + hidden * (1.0 - sig))


def tap_rows(acs, f, a):
    rows = (acs[f, 0:8, 0], acs[f, 0:8, 1], acs[f, 1:9, 0])[a]
    return rows.reshape(256, 384)


def encode(pairs, wd_ref):
    acc = None
    for acs, f, k in pairs:
        for a in range(3):
            term = dot(tap_rows(acs, f, a), wd_ref[3 * k + a])
            acc = term if acc is None else acc + term
    return acc.reshape(8, 32, 256)


def kernel_first(x_ref, m_ref, wconv_ref, wd_ref,
                 wc_ref, wa_ref, xs_ref, acs_ref, slope_ref, dact_ref, mt_ref, part_ref,
                 wide, ms):
    both_weights(wc_ref, wa_ref, wconv_ref, wd_ref)
    clear_edges(xs_ref, 4)
    for f in range(4):
        spread(xs_ref, f, *split_columns(wide.at[f % 2], x_ref[f]))
    for t in range(2):
        spread_out(ms, t, m_ref[t])
        mt_ref[:, 256 * t : 256 * t + 256] = turned(m_ref[t].reshape(256, 256))
    for f in range(2):
        hidden = conv_frame([xs_ref.at[f + k] for k in range(3)], wc_ref)
        slope_ref[f] = activate(hidden, acs_ref, f)
    part_ref[0] = encode(((acs_ref, 0, 0), (acs_ref, 1, 1)), wd_ref).astype(BF)
    even, odd = up_terms(ms, 0, 2, wa_ref)
    even_b, odd_b = up_terms(ms, 1, 0, wa_ref)
    dact_ref[0, :, 0] = even + even_b
    dact_ref[0, :, 1] = odd + odd_b
    for f, k in ((1, 1), (2, 2)):
        even, odd = up_terms(ms, 1, k, wa_ref)
        dact_ref[f, :, 0] = even
        dact_ref[f, :, 1] = odd


def call_first(x, m, w_conv, w_down):
    return pl.pallas_call(
        kernel_first,
        out_shape=(
            jax.ShapeDtypeStruct((9, 512, 256), BF),
            jax.ShapeDtypeStruct((9, 512, 256), BF),
            jax.ShapeDtypeStruct((4, 18, 32, 512), BF),
            jax.ShapeDtypeStruct((2, 9, 2, 32, 384), BF),
            jax.ShapeDtypeStruct((2, 512, 256), F32),
            jax.ShapeDtypeStruct((3, 8, 2, 32, 256), F32),
            jax.ShapeDtypeStruct((256, 512), BF),
            jax.ShapeDtypeStruct((1, 8, 32, 256), BF),
        ),
        in_specs=[VMEM] * 4,
        out_specs=(VMEM,) * 8,
        scratch_shapes=[
            pltpu.VMEM((2, 16, 64, 128), F32),
            pltpu.VMEM((2, 9, 32, 512), BF),
        ],
        compiler_params=params(12),
        cost_estimate=cost(10**6, 10**6),
    )(x, m, w_conv, w_down)


def kernel_grads(core_ref, before_ref, next_ref, wc_ref, wa_ref, wd_ref, xs_ref, high_ref, slope_ref, dact_ref, mt_ref,
                 hg_ref, own_ref, other_ref, even_ref, odd_ref,
                 wide, ms, up, hgt, low, xb, mn, sums, sems):
    core = core_ref[0]
    sums[0, HALF - 128 :] = jnp.zeros((128, 128), BF)
    sums[1, HALF - 256 :] = jnp.zeros((256, 128), BF)
    clear_edges(xb, 2)
    for f in range(2):
        spread(xb, f, *split_columns(wide.at[f], before_ref[f]))
    spread_out(ms, 0, next_ref[0])
    mn[...] = turned(next_ref[0].reshape(256, 256))
    for k in range(2):
        even, odd = up_terms(ms, 0, k, wa_ref)
        up[k, :, 0] = even
        up[k, :, 1] = odd
    every = [xb.at[f] for f in range(2)] + [xs_ref.at[f] for f in range(2)]
    for f in (2, 3, 0, 1):
        if f < 2:
            slope = activate(conv_frame(every[f : f + 3], wc_ref), low, f)
            grad = dact_ref[f].reshape(512, 256) * slope
        elif f == 2:
            grad = (dact_ref[2] + up[0]).reshape(512, 256) * slope_ref[0]
        else:
            grad = up[1].reshape(512, 256) * slope_ref[1]
        hg_ref[f] = grad.astype(BF).reshape(16, 32, 256)
        hgt[:, 512 * f : 512 * f + 512] = grad.T.astype(BF)

    def put(half, block, v):
        sums[half, 128 * block : 128 * block + 128] = v

    for k in range(3):
        left = mt_ref[...] if k == 2 else jnp.concatenate([mt_ref[:, 256:512], mn[...]], axis=1)
        f = 1 if k == 1 else 0
        for a in range(3):
            right = jnp.concatenate([tap_rows(low, f, a), tap_rows(high_ref, f, a)], axis=0)
            g = dot(left, right)
            for b in range(3):
                block = g[:, 128 * b : 128 * b + 128].T.astype(BF)
                at = 9 * k + 3 * a + b
                half, first = (0, 27 + 2 * at) if at < EARLY else (1, 2 * (at - EARLY))
                put(half, first, block[:, 0:128])
                put(half, first + 1, block[:, 128:256])

    for k in range(3):
        for a in range(3):
            right = xs_ref[0 : k + 2, a : a + 16].reshape(512 * (k + 2), 512)
            if k < 2:
                first = xb[k:2, a : a + 16].reshape(512 * (2 - k), 512)
                right = jnp.concatenate([first, right], axis=0)
            g = dot(hgt[...], right)
            for b in range(3):
                u, v = (2, 0, 1)[b], (0, 1, 3)[b]
                both = g[0:128, 128 * u : 128 * u + 128] + g[128:256, 128 * v : 128 * v + 128]
                put(0, 9 * k + 3 * a + b, both.T.astype(BF))

    send = pltpu.make_async_copy(sums.at[1 - core], other_ref, sems.at[0])
    keep = pltpu.make_async_copy(sums.at[core], own_ref, sems.at[1])
    send.start()
    keep.start()
    even_ref[...] = encode(((low, 0, 2),), wd_ref)
    pairs = ((low, 0, 0), (low, 1, 1), (high_ref, 0, 2))
    odd_ref[...] = encode(pairs, wd_ref).astype(BF)
    send.wait()
    keep.wait()


def call_grads(core, before, after, wc, wa, wd, xs, high, slope, dact, mt):
    return pl.pallas_call(
        kernel_grads,
        out_shape=(
            jax.ShapeDtypeStruct((4, 16, 32, 256), BF),
            jax.ShapeDtypeStruct((HALF, 128), BF),
            jax.ShapeDtypeStruct((HALF, 128), BF),
            jax.ShapeDtypeStruct((8, 32, 256), F32),
            jax.ShapeDtypeStruct((8, 32, 256), BF),
        ),
        in_specs=[SMEM] + [VMEM] * 10,
        out_specs=(VMEM, ANY, ANY, VMEM, VMEM),
        scratch_shapes=[
            pltpu.VMEM((2, 16, 64, 128), F32),
            pltpu.VMEM((1, 9, 32, 512), BF),
            pltpu.VMEM((2, 8, 2, 32, 256), F32),
            pltpu.VMEM((256, 2048), BF),
            pltpu.VMEM((2, 9, 2, 32, 384), BF),
            pltpu.VMEM((2, 18, 32, 512), BF),
            pltpu.VMEM((256, 256), BF),
            pltpu.VMEM((2, HALF, 128), BF),
            pltpu.SemaphoreType.DMA((2,)),
        ],
        compiler_params=params(24),
        cost_estimate=cost(10**6, 10**6),
    )(core, before, after, wc, wa, wd, xs, high, slope, dact, mt)


def kernel_clip(h_ref, after_ref, w_ref, even_ref, odd_ref, part_ref,
                out_ref, enc_ref, hs, wt, wide):
    enc_ref[0] = (even_ref[...] + part_ref[0].astype(F32)).astype(BF)
    enc_ref[1] = odd_ref[...]
    clear_edges(hs, 6)
    for tap in range(9):
        pair_weights(wt, tap, [turned(w_ref[3 * (8 - tap) + 2 - b]) for b in range(3)])
    for f in range(6):
        v = (h_ref[f] if f < 4 else after_ref[f - 4]).astype(F32)
        spread(hs, f, v[:, :, 0:128], v[:, :, 128:256])
    for f in range(4):
        v = conv_frame([hs.at[f + k] for k in range(3)], wt).reshape(16, 32, 256)
        wide[f % 2, :, pl.ds(0, 32, stride=2), :] = v[:, :, 0:128]
        wide[f % 2, :, pl.ds(1, 32, stride=2), :] = v[:, :, 128:256]
        out_ref[f] = wide[f % 2].astype(BF)


def call_clip(h, after, w, even, odd, part):
    return pl.pallas_call(
        kernel_clip,
        out_shape=(
            jax.ShapeDtypeStruct((4, 16, 64, 128), BF),
            jax.ShapeDtypeStruct((2, 8, 32, 256), BF),
        ),
        in_specs=[VMEM] * 6,
        out_specs=(VMEM, VMEM),
        scratch_shapes=[
            pltpu.VMEM((6, 18, 32, 512), BF),
            pltpu.VMEM((9, 512, 256), BF),
            pltpu.VMEM((2, 16, 64, 128), F32),
        ],
        compiler_params=params(32),
        cost_estimate=cost(5 * 10**9, 5 * 10**6),
    )(h, after, w, even, odd, part)


def write_half(half, scale, src, conv_ref, down_ref, conv, down, sems):
    def block(at):
        return src[128 * at : 128 * at + 128].astype(F32) * scale

    @pl.when(half == 0)
    def _():
        for at in range(27):
            conv[at] = block(at)
        to_conv = pltpu.make_async_copy(conv, conv_ref, sems.at[0])
        to_conv.start()
        for at in range(EARLY):
            down[at, :, 0:128] = block(27 + 2 * at)
            down[at, :, 128:256] = block(28 + 2 * at)
        to_down = pltpu.make_async_copy(down.at[0:EARLY], down_ref.at[0:EARLY], sems.at[1])
        to_down.start()
        to_conv.wait()
        to_down.wait()

    @pl.when(half == 1)
    def _():
        pieces = ((0, 7), (7, 14), (14, 27 - EARLY))
        copies = []
        for i, (first, last) in enumerate(pieces):
            for at in range(first, last):
                down[at, :, 0:128] = block(2 * at)
                down[at, :, 128:256] = block(2 * at + 1)
            target = down_ref.at[EARLY + first : EARLY + last]
            copies.append(pltpu.make_async_copy(down.at[first:last], target, sems.at[i]))
            copies[-1].start()
        for copy in copies:
            copy.wait()


def kernel_own(scale, core_ref, src, conv_ref, down_ref, conv, down, sems):
    write_half(core_ref[0], scale, src, conv_ref, down_ref, conv, down, sems)


def kernel_other(scale, core_ref, src, conv_in, down_in, conv_ref, down_ref, conv, down, sems):
    write_half(1 - core_ref[0], scale, src, conv_ref, down_ref, conv, down, sems)


def call_out(kernel, core, half, scale, begun=()):
    return pl.pallas_call(
        functools.partial(kernel, scale),
        out_shape=(pltpu.HBM((27, 128, 128), F32), pltpu.HBM((27, 128, 256), F32)),
        in_specs=[SMEM, VMEM] + [HBM] * len(begun),
        out_specs=(HBM, HBM),
        input_output_aliases={2: 0, 3: 1} if begun else {},
        scratch_shapes=[
            pltpu.VMEM((27, 128, 128), F32),
            pltpu.VMEM((27 - EARLY, 128, 256), F32),
            pltpu.SemaphoreType.DMA((3,)),
        ],
        compiler_params=params(16),
        cost_estimate=cost(10**6, 4 * 10**6),
    )(core, half, *begun)


CHUNK = HALF // 32


def kernel_fold(in_ref, out_ref):
    total = in_ref[0].astype(F32)
    for i in range(1, in_ref.shape[0]):
        total += in_ref[i].astype(F32)
    total = total.astype(BF)
    for i in range(out_ref.shape[0]):
        out_ref[i] = total


def call_fold(v, copies):
    return pl.pallas_call(
        kernel_fold,
        out_shape=jax.ShapeDtypeStruct((copies, CHUNK, 128), BF),
        in_specs=[VMEM],
        out_specs=VMEM,
        compiler_params=params(8),
        cost_estimate=cost(10**6, 10**6),
    )(v)


def shifted(block, distance):
    devices = range(8)
    route = [(i - distance, i) for i in devices if i - distance in devices]
    return lax.ppermute(block, TM, route)


def swapped(block):
    return lax.ppermute(block, "c", [(0, 1), (1, 0)])


def exchange(value, axes):
    return lax.all_to_all(value, axes, 0, 0, tiled=True)


def shards(clips, cotangent, clip_frames, w_conv, w_down):
    frames, rows, cols = clips.shape[1:4]
    core = lax.axis_index("c").astype(jnp.int32).reshape(1)
    last = clips[0, 2:]
    before = shifted(last, 1)
    cotangent, _ = lax.optimization_barrier((cotangent, last))
    times = lax.axis_index(TM) * 2 + jnp.arange(2, dtype=jnp.int32)
    keep = (2 * times < clip_frames[0])[:, None, None, None]
    masked = jnp.where(keep, cotangent[0], jnp.zeros_like(cotangent[0]))
    masked_after = shifted(masked[:1], -1)
    taps_conv = w_conv.reshape(27, 128, 128)
    taps_down = w_down.reshape(9, 384, 256)
    wc, wa, xs, high, slope, dact, mt, part = call_first(clips[0], masked, taps_conv, taps_down)
    hg, own, other, even, odd = call_grads(
        core, before, masked_after, wc, wa, taps_down, xs, high, slope, dact, mt
    )
    own = (own.astype(F32) + swapped(other).astype(F32)).astype(BF)
    own, part = lax.optimization_barrier((own, part))
    part = shifted(part, 1)
    own = exchange(own.reshape(32, CHUNK, 128), NEAR)
    own, part = lax.optimization_barrier((own, part))
    own = call_fold(own, 4)
    own, ends = lax.optimization_barrier((own, hg[:2]))
    after = shifted(ends, -1)
    own = call_fold(exchange(own, "zh"), 32)
    own, after = lax.optimization_barrier((own, after))
    own = exchange(own, NEAR).reshape(HALF, 128)
    clip_grad, encoded = call_clip(hg, after, taps_conv, even, odd, part)
    own, clip_grad, encoded = lax.optimization_barrier((own, clip_grad, encoded))
    scale = 1.0 / math.sqrt(lax.axis_size(DP) * frames * lax.axis_size(TM) * rows * cols)
    begun = call_out(kernel_own, core, own, scale)
    conv_grad, down_grad = call_out(kernel_other, core, swapped(own), scale, begun)
    return (encoded[None], clip_grad[None], conv_grad.reshape(w_conv.shape), down_grad.reshape(w_down.shape))


def solution(mesh):
    fine = Mesh(mesh.devices.reshape(2, 4, 2, 2, 4, 2), DP + TM)
    parts = P(DP, TM, None, None, None)
    in_specs = (parts, parts, P(DP), P(), P())
    out_specs = (parts, parts, P(), P())
    return jax.shard_map(shards, mesh=fine, in_specs=in_specs, out_specs=out_specs, check_vma=False)
```
